128 devices in a mesh: dev: 128 (over y, z, x, core).
Axes of the slice: x: 4, y: 4, z: 4, core: 2. Of those that a mesh axis runs over, the one named last changes fastest.
Arguments:
- vectors: bfloat16 [131072, 768], P('dev'), may hold values from -6 to 6
- row_list: int32 [131072], P('dev'), may hold values from 0 to 511
- block_owner: int32 [4096], P('dev'), may hold values from 0 to 127, as said below
- block_fill: int32 [4096], P('dev'), may hold values from 1 to 32
- old_centroids: float32 [65536, 768], P('dev'), may hold values from -6 to 6
- codebook: bfloat16 [24, 32, 256], replicated, may hold values from -6 to 6
Outputs:
- new_centroids: float32 [65536, 768], P('dev')
- slot_error: float32 [16384, 32], P('dev')
- sub_covariance: float32 [24, 32, 32], replicated
The draws below stay inside these ranges and needn't reach their ends.
Inputs may be any that keep to these rules, and one draw needn't show every extreme that they name: `block_owner`: the blocks of one device go to distinct owners, and in every draw some owner receives one block from every device.
All inputs are finite; a program needn't handle non-finite values.
Results may differ from the reference program's by a relative error of at most 0.0003.
Values may be sent and summed in bfloat16 or wider, within the bound.
No kernel may reach another device: no remote copies, remote signals or barrier semaphores. Data moves between devices by JAX's collectives and lax.ppermute only.
A program may use at most 128 MiB of HBM per device.

```python
import jax
import jax.numpy as jnp
from jax import lax

D = 768
M = 24
DSUB = 32
KSUB = 256
LIST_DEV = 512
LISTS = 65536
BLK = 32
BLK_DEV = 32
BLOCKS = 4096
ROWS = 131072
SLOTS = 16384
N_DEV = 128


def draw_block_owner(key, part):
    key = jax.random.fold_in(key, 11)
    hot_count = max(1, BLK_DEV // 4)
    cold_count = BLK_DEV - hot_count
    owners = jax.random.permutation(jax.random.fold_in(key, 1), N_DEV).astype(jnp.int32)
    starts = jax.random.randint(jax.random.fold_in(key, 2), (N_DEV,), 0, N_DEV - hot_count).astype(jnp.int32)
    hot_part = jnp.broadcast_to(owners[:hot_count][None, :], (N_DEV, hot_count))
    shifts = (starts[:, None] + jnp.arange(cold_count, dtype=jnp.int32)[None, :]) % (N_DEV - hot_count)
    cold_part = owners[hot_count + shifts]
    chosen = jnp.concatenate([hot_part, cold_part], axis=1).astype(jnp.int32)
    scores = jax.random.randint(jax.random.fold_in(key, 3), (N_DEV, BLK_DEV), 0, 2 ** 20) * BLK_DEV + jnp.arange(BLK_DEV, dtype=jnp.int32)[None, :]
    ranks = jnp.argsort(scores, axis=1, stable=True)
    chosen = jnp.take_along_axis(chosen, ranks, axis=1)
    return chosen.reshape(N_DEV * BLK_DEV).astype(jnp.int32)


def place_ends(result, stream_key, low, top_value):
    extent = result.shape
    index_at = [jax.random.randint(jax.random.fold_in(stream_key, axis), (), 0, extent[axis]) for axis in range(len(extent))]
    result = result.at[tuple(index_at)].set(low)
    longest = extent.index(max(extent))
    index_at[longest] = (index_at[longest] + 1) % extent[longest]
    return result.at[tuple(index_at)].set(top_value)


def steps_of(rng, shape, cuts, low, high):
    loudness, own = 1.0, jax.random.fold_in(rng, 6)
    for axis_at, parts in cuts:
        draws = jnp.exp(jax.random.uniform(jax.random.fold_in(own, axis_at), (parts,), jnp.float32, low / len(cuts), high / len(cuts)))
        loudness = loudness * jnp.repeat(draws, shape[axis_at] // parts).reshape([-1 if axis == axis_at else 1 for axis in range(len(shape))])
    return loudness


def bell_draw(key, extent, deviation, reach, cuts=(), kind=jnp.bfloat16):
    result = jax.random.normal(key, extent, jnp.float32) * deviation
    if len(cuts) > 0:
        result = steps_of(key, extent, cuts, -0.22, 0.18) * result
    return jnp.clip(result, min=-reach, max=reach).astype(kind)


def setup_inputs(seed: int = 0) -> dict:
    keys = jax.random.split(jax.random.key(seed), 7)
    return {
        "vectors": bell_draw(keys[0], (ROWS, D), 1.0, 6.0, ((0, 128),)),
        "row_list": place_ends(jax.random.randint(keys[1], (ROWS,), 0, LIST_DEV), jax.random.fold_in(keys[1], 1), 0, LIST_DEV - 1).astype(jnp.int32),
        "block_owner": draw_block_owner(jax.random.fold_in(keys[6], 71), 0),
        "block_fill": place_ends(jax.random.randint(keys[3], (BLOCKS,), 1, BLK + 1), jax.random.fold_in(keys[3], 1), 1, BLK).astype(jnp.int32),
        "old_centroids": bell_draw(keys[4], (LISTS, D), 1.0, 6.0, ((0, 128),), jnp.float32),
        "codebook": bell_draw(keys[5], (M, DSUB, KSUB), 1.0, 6.0),
    }


def quantize_terms(residual, codebook, weights_here):
    row_count = residual.shape[0]
    pieces = residual.astype(jnp.float32).reshape(row_count, M, DSUB)
    book_values = codebook.astype(jnp.float32)
    cross_terms = jnp.einsum("rmd,mdk->rmk", pieces, book_values)
    row_norm = jnp.sum(pieces * pieces, axis=2)
    book_norm = jnp.sum(book_values * book_values, axis=1)
    distance = row_norm[:, :, None] - 2.0 * cross_terms + book_norm[None, :, :]
    row_error = jnp.sum(jnp.min(distance, axis=2), axis=1) / D * weights_here
    moment = jnp.einsum("rmd,rme->mde", pieces, pieces)
    return row_error, moment


def reference(vectors, row_list, block_owner, block_fill, old_centroids, codebook):
    offsets = jnp.arange(BLK, dtype=jnp.int32)
    weights = (offsets[None, :] < block_fill[:, None]).astype(jnp.float32)
    global_list = (block_owner[:, None] * LIST_DEV + row_list.reshape(BLOCKS, BLK)).astype(jnp.int32)
    source_rows = vectors.reshape(N_DEV, BLK_DEV * BLK, D)
    source_lists = global_list.reshape(N_DEV, BLK_DEV * BLK)
    source_weights = weights.reshape(N_DEV, BLK_DEV * BLK)

    def accumulate(carry, inputs_here):
        list_sums, counts = carry
        rows_here, lists_here, weights_here = inputs_here
        list_sums = list_sums + jax.ops.segment_sum(rows_here.astype(jnp.float32) * weights_here[:, None], lists_here, num_segments=LISTS)
        counts = counts + jax.ops.segment_sum(weights_here, lists_here, num_segments=LISTS)
        return (list_sums, counts), None

    start_state = (jnp.zeros((LISTS, D), jnp.float32), jnp.zeros((LISTS,), jnp.float32))
    (list_sums, counts), unused = lax.scan(accumulate, start_state, (source_rows, source_lists, source_weights))
    centroids = (list_sums + old_centroids) / (counts + 1.0)[:, None]

    def encode(carry, inputs_here):
        rows_here, lists_here, weights_here = inputs_here
        residual = ((rows_here.astype(jnp.float32) - centroids[lists_here]) * weights_here[:, None]).astype(jnp.bfloat16)
        residual = lax.optimization_barrier(residual)
        row_error, moment = quantize_terms(residual, codebook, weights_here)
        return carry + moment, row_error

    moments, errors = lax.scan(encode, jnp.zeros((M, DSUB, DSUB), jnp.float32), (source_rows, source_lists, source_weights))
    errors = errors.reshape(BLOCKS, BLK)
    source_of = (jnp.arange(BLOCKS, dtype=jnp.int32) // BLK_DEV).astype(jnp.int32)
    slot_index = (block_owner * N_DEV + source_of).astype(jnp.int32)
    slot_error = jnp.zeros((SLOTS, BLK), jnp.float32).at[slot_index].set(errors)
    total_weight = jnp.sum(block_fill.astype(jnp.float32))
    return centroids, slot_error, moments / total_weight
```

```python
import functools

import jax
import jax.numpy as jnp
from jax import lax
from jax.experimental import pallas as pl
from jax.experimental.pallas import tpu as pltpu
from jax.sharding import PartitionSpec as P

LANES = 128
META = 16
AUG = 16
GROUP = 512
VMEM = 56 * 1024 * 1024


def send_kernel(blk, owner_ref, fill_ref, vec_ref, list_ref, send_ref, tiles, meta, sems):
    blocks = owner_ref.shape[0]
    width = vec_ref.shape[1]
    chunks = width // LANES
    span = LANES // blk
    place = lax.rem(lax.axis_index("dev"), span)
    for j in range(chunks):
        tiles[:, j * blk : (j + 1) * blk, :] = vec_ref[:, j * LANES : (j + 1) * LANES].reshape(
            blocks, blk, LANES
        )
    copies = []
    for b in range(blocks):
        copy = pltpu.make_async_copy(
            tiles.at[b], send_ref.at[owner_ref[b], pl.ds(0, chunks * blk), :], sems.at[b]
        )
        copy.start()
        copies.append(copy)
    total = functools.reduce(lambda a, b: a + b, [fill_ref[b] for b in range(blocks)])
    rows = lax.broadcasted_iota(jnp.int32, (META, LANES), 0)
    lane = lax.broadcasted_iota(jnp.int32, (1, LANES), 1)
    base = jnp.where(rows == 3, total >> 8, jnp.where(rows == 4, total & 255, 0))
    meta[...] = jnp.broadcast_to(base.astype(jnp.float32).astype(jnp.bfloat16)[None], meta.shape)
    for b in range(blocks):
        line = list_ref[b // span : b // span + 1, :] + 1
        line = pltpu.roll(line, lax.rem(place + span - b % span, span) * blk, 1)
        kept = (lane // blk == place) & (lax.rem(lane, blk) < fill_ref[b])
        line = jnp.broadcast_to(jnp.where(kept, line, 0), (META, LANES))
        tile = jnp.where(
            rows == 0, line & 255, jnp.where(rows == 1, line >> 8, jnp.where(rows == 2, 1, base))
        )
        meta[owner_ref[b]] = tile.astype(jnp.float32).astype(jnp.bfloat16)
    last = pltpu.make_async_copy(
        meta, send_ref.at[:, pl.ds(chunks * blk, META), :], sems.at[blocks]
    )
    last.start()
    for copy in copies:
        copy.wait()
    last.wait()


def build_send(vectors, row_list, block_owner, block_fill, devices):
    rows, width = vectors.shape
    blocks = block_owner.shape[0]
    blk = rows // blocks
    height = width // LANES * blk
    return pl.pallas_call(
        functools.partial(send_kernel, blk),
        out_shape=jax.ShapeDtypeStruct((devices, height + META, LANES), jnp.bfloat16),
        in_specs=[
            pl.BlockSpec(memory_space=pltpu.SMEM),
            pl.BlockSpec(memory_space=pltpu.SMEM),
            pl.BlockSpec(memory_space=pltpu.VMEM),
            pl.BlockSpec(memory_space=pltpu.VMEM),
        ],
        out_specs=pl.BlockSpec(memory_space=pl.ANY),
        scratch_shapes=[
            pltpu.VMEM((blocks, height, LANES), jnp.bfloat16),
            pltpu.VMEM((devices, META, LANES), jnp.bfloat16),
            pltpu.SemaphoreType.DMA((blocks + 1,)),
        ],
        compiler_params=pltpu.CompilerParams(vmem_limit_bytes=VMEM),
        name="build_send",
    )(block_owner, block_fill, vectors, row_list.reshape(rows // LANES, LANES))


def update_kernel(
    blk, recv_ref, old_ref, cent_ref, resid_ref, code_ref, mom_ref, total_ref,
    hot, turned, codes, sums, counts, high, low, gram, tot,
):
    step = pl.program_id(0)
    groups = pl.num_programs(0) // 2
    slots = recv_ref.shape[0]
    lists, width = old_ref.shape
    chunks = width // LANES
    span = LANES // blk

    @pl.when(step == 0)
    def _():
        sums[...] = jnp.zeros_like(sums)
        counts[...] = jnp.zeros_like(counts)
        tot[...] = jnp.zeros_like(tot)

    @pl.when(step < groups)
    def _():
        lines = []
        pieces = [[] for _ in range(chunks)]
        seen = jnp.zeros((1, LANES), jnp.float32)
        for s in range(slots):
            info = recv_ref[s, chunks * blk : chunks * blk + META, :].astype(jnp.float32)
            line = info[0:1] + 256.0 * info[1:2]
            if s % span == 0:
                lines.append(line)
            else:
                lines[-1] = lines[-1] + line
            seen = seen + (info[4:5] + 256.0 * info[3:4])
            there = jnp.broadcast_to(info[2:3], (blk, LANES)) > 0.0
            for j in range(chunks):
                piece = recv_ref[s, j * blk : (j + 1) * blk, :].astype(jnp.float32)
                pieces[j].append(jnp.where(there, piece, 0.0).astype(jnp.bfloat16))
        tot[...] += seen
        code = jnp.concatenate(lines, axis=1)
        codes[step] = jnp.broadcast_to(code, codes.shape[1:])
        ids = lax.broadcasted_iota(jnp.int32, (lists, GROUP), 0).astype(jnp.float32) + 1.0
        match = jnp.where(ids == code, 1.0, 0.0)
        chosen = match.astype(jnp.bfloat16)
        hot[step] = chosen
        part = match[:, 0:LANES]
        for k in range(1, GROUP // LANES):
            part = part + match[:, k * LANES : (k + 1) * LANES]
        counts[...] += part
        for j in range(chunks):
            column = jnp.concatenate(pieces[j], axis=0)
            turned[step, j * LANES : (j + 1) * LANES, :] = column.T
            pieces[j] = column
        values = jnp.concatenate(pieces, axis=1)
        sums[...] += jnp.dot(chosen, values, preferred_element_type=jnp.float32)

    @pl.when(step == groups)
    def _():
        count = jnp.sum(counts[...], axis=1, keepdims=True) + 1.0
        cent = (sums[...] + old_ref[...]) / count
        cent_ref[...] = cent
        flipped = cent.T
        head = flipped.astype(jnp.bfloat16)
        high[...] = head
        low[...] = (flipped - head.astype(jnp.float32)).astype(jnp.bfloat16)
        gram[...] = jnp.zeros_like(gram)

    @pl.when(step >= groups)
    def _():
        now = step - groups
        chosen = hot[now]
        code = codes[now][0:1]
        weight = jnp.where(code > 0.0, 1.0, 0.0)
        code_ref[...] = jnp.broadcast_to(weight, code_ref.shape)
        wide = 2 * LANES
        for j in range(width // wide):
            at = slice(j * wide, (j + 1) * wide)
            picked = jnp.dot(high[at], chosen, preferred_element_type=jnp.float32)
            picked = picked + jnp.dot(low[at], chosen, preferred_element_type=jnp.float32)
            resid = ((turned[now, at].astype(jnp.float32) - picked) * weight).astype(jnp.bfloat16)
            resid_ref[0, at] = resid
            gram[j] += lax.dot_general(
                resid, resid, (((1,), (1,)), ((), ())), preferred_element_type=jnp.float32
            )

    @pl.when(step == 2 * groups - 1)
    def _():
        sub = mom_ref.shape[1]
        across = LANES // sub
        lane = lax.broadcasted_iota(jnp.int32, (sub, LANES), 1)
        for q in range(chunks):
            half = slice((q % 2) * LANES, (q % 2 + 1) * LANES)
            line = jnp.zeros((sub, LANES), jnp.float32)
            for a in range(across):
                top = ((q % 2) * across + a) * sub
                line = jnp.where(lane // sub == a, gram[q // 2, top : top + sub, half], line)
            mom_ref[q] = line
        total_ref[...] = jnp.broadcast_to(tot[...], total_ref.shape)


def update_lists(recv, old, blk, sub):
    slots, height, _ = recv.shape
    lists, width = old.shape
    rows = slots * blk
    groups = rows // GROUP
    each = GROUP // blk
    return pl.pallas_call(
        functools.partial(update_kernel, blk),
        grid=(2 * groups,),
        out_shape=(
            jax.ShapeDtypeStruct((lists, width), jnp.float32),
            jax.ShapeDtypeStruct((groups, width, GROUP), jnp.bfloat16),
            jax.ShapeDtypeStruct((groups, 8, GROUP), jnp.float32),
            jax.ShapeDtypeStruct((width // LANES, sub, LANES), jnp.float32),
            jax.ShapeDtypeStruct((8, LANES), jnp.float32),
        ),
        in_specs=[
            pl.BlockSpec((each, height, LANES), lambda i: (jnp.minimum(i, groups - 1), 0, 0)),
            pl.BlockSpec((lists, width), lambda i: (0, 0)),
        ],
        out_specs=(
            pl.BlockSpec((lists, width), lambda i: (0, 0)),
            pl.BlockSpec((1, width, GROUP), lambda i: (jnp.maximum(i - groups, 0), 0, 0)),
            pl.BlockSpec((1, 8, GROUP), lambda i: (jnp.maximum(i - groups, 0), 0, 0)),
            pl.BlockSpec((width // LANES, sub, LANES), lambda i: (0, 0, 0)),
            pl.BlockSpec((8, LANES), lambda i: (0, 0)),
        ),
        scratch_shapes=[
            pltpu.VMEM((groups, lists, GROUP), jnp.bfloat16),
            pltpu.VMEM((groups, width, GROUP), jnp.bfloat16),
            pltpu.VMEM((groups, 8, GROUP), jnp.float32),
            pltpu.VMEM((lists, width), jnp.float32),
            pltpu.VMEM((lists, LANES), jnp.float32),
            pltpu.VMEM((width, lists), jnp.bfloat16),
            pltpu.VMEM((width, lists), jnp.bfloat16),
            pltpu.VMEM((width // (2 * LANES), 2 * LANES, 2 * LANES), jnp.float32),
            pltpu.VMEM((1, LANES), jnp.float32),
        ],
        compiler_params=pltpu.CompilerParams(vmem_limit_bytes=VMEM),
        name="update_lists",
    )(recv, old)


def error_kernel(sub, resid_ref, weight_ref, book_ref, error_ref):
    subspaces = book_ref.shape[0]
    ones = jnp.ones((AUG, GROUP), jnp.bfloat16)
    norm = jnp.zeros((8, GROUP), jnp.float32)
    least = jnp.zeros((1, GROUP), jnp.float32)
    for m in range(subspaces):
        piece = resid_ref[0, m * sub : (m + 1) * sub, :]
        long = piece.astype(jnp.float32)
        square = long * long
        for k in range(sub // 8):
            norm = norm + square[k * 8 : (k + 1) * 8]
        distance = jnp.dot(
            book_ref[m],
            jnp.concatenate([piece, ones], axis=0),
            preferred_element_type=jnp.float32,
        )
        least = least + jnp.min(distance, axis=0, keepdims=True)
    width = subspaces * sub
    error = (least + jnp.sum(norm, axis=0, keepdims=True)) * (weight_ref[0, 0:1] / width)
    error_ref[0] = jnp.broadcast_to(error, error_ref.shape[1:])


def row_errors(resid, weight, book, sub, first, count):
    groups, width, _ = resid.shape
    subspaces, codes, depth = book.shape
    return pl.pallas_call(
        functools.partial(error_kernel, sub),
        grid=(count,),
        out_shape=jax.ShapeDtypeStruct((count, 8, GROUP), jnp.float32),
        in_specs=[
            pl.BlockSpec((1, width, GROUP), lambda i: (first + i, 0, 0)),
            pl.BlockSpec((1, 8, GROUP), lambda i: (first + i, 0, 0)),
            pl.BlockSpec((subspaces, codes, depth), lambda i: (0, 0, 0)),
        ],
        out_specs=pl.BlockSpec((1, 8, GROUP), lambda i: (i, 0, 0)),
        compiler_params=pltpu.CompilerParams(vmem_limit_bytes=VMEM),
        cost_estimate=pl.CostEstimate(
            flops=2 * 256 * codes * subspaces * GROUP * count,
            bytes_accessed=width * GROUP * count * 2,
            transcendentals=0,
        ),
        name="row_errors",
    )(resid, weight, book)


def extended_book(codebook):
    values = codebook.astype(jnp.float32)
    rest = jnp.sum(jnp.square(values), axis=1)
    parts = []
    for _ in range(3):
        part = lax.reduce_precision(rest, 8, 7)
        parts.append(part)
        rest = rest - part
    parts = jnp.stack(parts, axis=2)
    parts = jnp.pad(parts, ((0, 0), (0, 0), (0, AUG - 3)))
    return jnp.concatenate([-2.0 * values.transpose(0, 2, 1), parts], axis=2).astype(jnp.bfloat16)


def body(vectors, row_list, block_owner, block_fill, old_centroids, codebook):
    devices = lax.axis_size("dev")
    blk = row_list.shape[0] // block_owner.shape[0]
    sub = codebook.shape[1]
    width = vectors.shape[1]
    book = extended_book(codebook)
    send = build_send(vectors, row_list, block_owner, block_fill, devices)
    recv = lax.all_to_all(send, "dev", split_axis=0, concat_axis=0, tiled=True)
    centroids, resid, weight, moment, total = update_lists(recv, old_centroids, blk, sub)

    half = moment.shape[0] // 2
    first, second = moment[:half], moment[half:]
    row = lax.broadcasted_iota(jnp.int32, first.shape, 1)
    column = lax.broadcasted_iota(jnp.int32, first.shape, 2) % sub
    diagonal = jnp.sum(jnp.where(row == column, second, 0.0), axis=1)
    packed = jnp.concatenate(
        [
            jnp.where(row <= column, first, second).reshape(half * sub, LANES),
            jnp.pad(diagonal, ((0, 8 - half), (0, 0))),
        ],
        axis=0,
    )
    stride = 1
    while stride < devices:
        pairs = [(i, i ^ stride) for i in range(devices)]
        packed = packed + lax.ppermute(packed, "dev", pairs)
        stride *= 2
    groups = resid.shape[0]
    parts = 4
    errors = [
        row_errors(resid, weight, book, sub, p * groups // parts, groups // parts)
        for p in range(parts)
    ]
    slot_error = jnp.concatenate([e[:, 0, :] for e in errors], axis=0).reshape(devices, blk)
    across = LANES // sub
    upper = packed[: half * sub].reshape(half, sub, across, sub).transpose(0, 2, 1, 3)
    diagonal = packed[half * sub : half * sub + half].reshape(half, across, 1, sub)
    row = lax.broadcasted_iota(jnp.int32, upper.shape, 2)
    column = lax.broadcasted_iota(jnp.int32, upper.shape, 3)
    flipped = upper.transpose(0, 1, 3, 2)
    one = jnp.where(row <= column, upper, flipped)
    other = jnp.where(row > column, upper, jnp.where(row < column, flipped, diagonal))
    moments = jnp.concatenate([one, other], axis=0).reshape(2 * half * across, sub, sub)
    return centroids, slot_error, moments / total[0, 0]


def solution(mesh):
    return jax.shard_map(
        body,
        mesh=mesh,
        in_specs=(P("dev", None), P("dev"), P("dev"), P("dev"), P("dev", None), P()),
        out_specs=(P("dev", None), P("dev", None), P()),
        check_vma=False,
    )
```

```python
import functools

import jax
import jax.numpy as jnp
from jax import lax
from jax.experimental import pallas as pl
from jax.experimental.pallas import tpu as pltpu
from jax.sharding import PartitionSpec as P

LANES = 128
META = 16
AUG = 16
GROUP = 256
VMEM = 56 * 1024 * 1024


def send_kernel(blk, owner_ref, fill_ref, vec_ref, list_ref, send_ref, tiles, meta, sems):
    blocks = owner_ref.shape[0]
    width = vec_ref.shape[1]
    chunks = width // LANES
    span = LANES // blk
    me = lax.axis_index("dev")
    place = lax.rem(me, span)
    for j in range(chunks):
        tiles[:, j * blk : (j + 1) * blk, :] = vec_ref[:, j * LANES : (j + 1) * LANES].reshape(
            blocks, blk, LANES
        )
    copies = []
    for b in range(blocks):
        copy = pltpu.make_async_copy(
            tiles.at[b], send_ref.at[owner_ref[b], pl.ds(0, chunks * blk), :], sems.at[b]
        )
        copy.start()
        copies.append(copy)
    total = functools.reduce(lambda a, b: a + b, [fill_ref[b] for b in range(blocks)])
    rows = lax.broadcasted_iota(jnp.int32, (META, LANES), 0)
    lane = lax.broadcasted_iota(jnp.int32, (1, LANES), 1)
    base = jnp.where(rows == 3, total >> 8, jnp.where(rows == 4, total & 255, 0))
    meta[...] = jnp.broadcast_to(base.astype(jnp.float32).astype(jnp.bfloat16)[None], meta.shape)
    for b in range(blocks):
        line = list_ref[b // span : b // span + 1, :] + 1
        line = pltpu.roll(line, lax.rem(place + span - b % span, span) * blk, 1)
        kept = (lane // blk == place) & (lax.rem(lane, blk) < fill_ref[b])
        line = jnp.broadcast_to(jnp.where(kept, line, 0), (META, LANES))
        count = jnp.broadcast_to(jnp.where(lane == me, fill_ref[b], 0), (META, LANES))
        tile = jnp.where(
            rows == 0, line & 255, jnp.where(rows == 1, line >> 8, jnp.where(rows == 2, count, base))
        )
        meta[owner_ref[b]] = tile.astype(jnp.float32).astype(jnp.bfloat16)
    last = pltpu.make_async_copy(
        meta, send_ref.at[:, pl.ds(chunks * blk, META), :], sems.at[blocks]
    )
    last.start()
    for copy in copies:
        copy.wait()
    last.wait()


def build_send(vectors, row_list, block_owner, block_fill, devices):
    rows, width = vectors.shape
    blocks = block_owner.shape[0]
    blk = rows // blocks
    height = width // LANES * blk
    return pl.pallas_call(
        functools.partial(send_kernel, blk),
        out_shape=jax.ShapeDtypeStruct((devices, height + META, LANES), jnp.bfloat16),
        in_specs=[
            pl.BlockSpec(memory_space=pltpu.SMEM),
            pl.BlockSpec(memory_space=pltpu.SMEM),
            pl.BlockSpec(memory_space=pltpu.VMEM),
            pl.BlockSpec(memory_space=pltpu.VMEM),
        ],
        out_specs=pl.BlockSpec(memory_space=pl.ANY),
        scratch_shapes=[
            pltpu.VMEM((blocks, height, LANES), jnp.bfloat16),
            pltpu.VMEM((devices, META, LANES), jnp.bfloat16),
            pltpu.SemaphoreType.DMA((blocks + 1,)),
        ],
        compiler_params=pltpu.CompilerParams(vmem_limit_bytes=VMEM),
        name="build_send",
    )(block_owner, block_fill, vectors, row_list.reshape(rows // LANES, LANES))


def update_kernel(
    blk, recv_ref, old_ref, cent_ref, resid_ref, place_ref, packed_ref, total_ref,
    blocks, info, old, dense, hot, turned, column, where_ref, sums, counts, parts, gram, final, sems, out_sems,
):
    slots, height, _ = recv_ref.shape
    lists, width = old_ref.shape
    chunks = width // LANES
    span = LANES // blk
    some = slots // blocks.shape[0]
    rows = slots * blk

    notes = pltpu.make_async_copy(recv_ref.at[:, pl.ds(chunks * blk, META), :], info, sems.at[0])
    notes.start()

    def fetch(c):
        return pltpu.make_async_copy(
            recv_ref.at[pl.ds(c * some, some), pl.ds(0, chunks * blk), :], blocks.at[c], sems.at[1 + c]
        )

    for c in range(blocks.shape[0]):
        fetch(c).start()

    own = pltpu.make_async_copy(old_ref, old, sems.at[1 + blocks.shape[0]])
    own.start()
    notes.wait()
    lines, seen = [], jnp.zeros((META, LANES), jnp.float32)
    for q in range(slots // span):
        note = info[q * span].astype(jnp.float32)
        for s in range(1, span):
            note = note + info[q * span + s].astype(jnp.float32)
        lines.append(note[0:1] + 256.0 * note[1:2])
        seen = seen + note
    fill = jnp.broadcast_to(seen[2:3], (8, LANES))
    before = lax.broadcasted_iota(jnp.int32, (slots, slots), 0)
    after = lax.broadcasted_iota(jnp.int32, (slots, slots), 1)
    start = jnp.dot(
        fill.astype(jnp.bfloat16),
        jnp.where(before < after, 1.0, 0.0).astype(jnp.bfloat16),
        preferred_element_type=jnp.float32,
    )
    which = lax.broadcasted_iota(jnp.int32, (8, slots), 0)
    where_ref[...] = jnp.where(which == 0, start, fill).astype(jnp.int32)
    mover = pltpu.make_async_copy(where_ref, place_ref, sems.at[0])
    mover.start()
    total_ref[...] = jnp.broadcast_to(seen[4:5] + 256.0 * seen[3:4], total_ref.shape)
    lines.append(jnp.zeros((LANES - len(lines), LANES), jnp.float32))
    column[...] = jnp.concatenate(lines, axis=0).T
    sums[...] = jnp.zeros_like(sums)
    counts[...] = jnp.zeros_like(counts)
    gram[...] = jnp.zeros_like(gram)
    mover.wait()

    lane = lax.broadcasted_iota(jnp.int32, (blk, LANES), 1)

    def pack(c, carry):
        fetch(c).wait()
        for s in range(some):
            at = pl.ds(place_ref[0, c * some + s], blk)
            for j in range(chunks):
                dense[j, at, :] = blocks[c, s, j * blk : (j + 1) * blk, :].astype(jnp.float32)
            ids = column[(s % span) * blk : (s % span + 1) * blk, :]
            dense[chunks, at, :] = jnp.where(lane == c * (some // span) + s // span, ids, 0.0)
        return carry

    lax.fori_loop(0, blocks.shape[0], pack, 0)
    used = place_ref[0, slots - 1] + place_ref[1, slots - 1]
    for j in range(chunks + 1):
        dense[j, pl.ds(used, GROUP + blk), :] = jnp.zeros((GROUP + blk, LANES), jnp.float32)
    groups = (used + GROUP - 1) // GROUP

    def gather(g, carry):
        at = pl.ds(pl.multiple_of(g * GROUP, GROUP), GROUP)
        code = jnp.sum(dense[chunks, at, :].T, axis=0, keepdims=True)
        ids = lax.broadcasted_iota(jnp.int32, (lists, GROUP), 0).astype(jnp.float32) + 1.0
        match = jnp.where(ids == code, 1.0, 0.0)
        chosen = match.astype(jnp.bfloat16)
        hot[g] = chosen
        part = match[:, 0:LANES]
        for k in range(1, GROUP // LANES):
            part = part + match[:, k * LANES : (k + 1) * LANES]
        counts[...] += part
        pieces = []
        for j in range(chunks):
            piece = dense[j, at, :].astype(jnp.bfloat16)
            turned[g, j * LANES : (j + 1) * LANES, :] = piece.T
            pieces.append(piece)
        sums[...] += jnp.dot(
            chosen, jnp.concatenate(pieces, axis=1), preferred_element_type=jnp.float32
        )
        return carry

    lax.fori_loop(0, groups, gather, 0)

    count = jnp.sum(counts[...], axis=1, keepdims=True) + 1.0
    own.wait()
    cent = (sums[...] + old[...]) / count
    final[...] = cent
    write = pltpu.make_async_copy(final, cent_ref, sems.at[0])
    write.start()
    flipped = cent.T
    head = flipped.astype(jnp.bfloat16)
    parts[:, 0:lists] = head
    parts[:, lists : 2 * lists] = (flipped - head.astype(jnp.float32)).astype(jnp.bfloat16)

    wide = 2 * LANES
    lane = lax.broadcasted_iota(jnp.int32, (1, GROUP), 1)

    def leave(g):
        return pltpu.make_async_copy(turned.at[g], resid_ref.at[g], out_sems.at[g])

    def encode(g, carry):
        chosen = hot[g]
        weight = jnp.where(lane < used - g * GROUP, 1.0, 0.0)
        both = jnp.concatenate([chosen, chosen], axis=0)
        resids = []
        for j in range(width // wide):
            at = slice(j * wide, (j + 1) * wide)
            picked = jnp.dot(parts[at], both, preferred_element_type=jnp.float32)
            resids.append(((turned[g, at].astype(jnp.float32) - picked) * weight).astype(jnp.bfloat16))
        for j in range(width // wide):
            turned[g, j * wide : (j + 1) * wide] = resids[j]
        squares = [
            lax.dot_general(r, r, (((1,), (1,)), ((), ())), preferred_element_type=jnp.float32)
            for r in resids
        ]
        for j in range(width // wide):
            gram[j] += squares[j]
        leave(g).start()
        return carry

    lax.fori_loop(0, groups, encode, 0)

    sub = (packed_ref.shape[0] - 8) // (chunks // 2)
    across = LANES // sub
    row = lax.broadcasted_iota(jnp.int32, (sub, LANES), 0)
    lane = lax.broadcasted_iota(jnp.int32, (sub, LANES), 1)
    squares = []
    for q in range(chunks):
        half = slice((q % 2) * LANES, (q % 2 + 1) * LANES)
        square = jnp.zeros((sub, LANES), jnp.float32)
        for a in range(across):
            top = ((q % 2) * across + a) * sub
            square = jnp.where(lane // sub == a, gram[q // 2, top : top + sub, half], square)
        squares.append(square)
    half = chunks // 2
    diagonals = []
    for q in range(half):
        packed_ref[q * sub : (q + 1) * sub, :] = jnp.where(
            row <= lane % sub, squares[q], squares[half + q]
        )
        diagonals.append(
            jnp.sum(jnp.where(row == lane % sub, squares[half + q], 0.0), axis=0, keepdims=True)
        )
    diagonals.append(jnp.zeros((8 - half, LANES), jnp.float32))
    packed_ref[half * sub :, :] = jnp.concatenate(diagonals, axis=0)

    def finish(g, carry):
        leave(g).wait()
        return carry

    lax.fori_loop(0, groups, finish, 0)
    write.wait()


def update_lists(recv, old, blk, sub):
    slots, height, _ = recv.shape
    lists, width = old.shape
    rows = slots * blk
    groups = rows // GROUP
    chunks = width // LANES
    return pl.pallas_call(
        functools.partial(update_kernel, blk),
        out_shape=(
            jax.ShapeDtypeStruct((lists, width), jnp.float32),
            jax.ShapeDtypeStruct((groups, width, GROUP), jnp.bfloat16),
            jax.ShapeDtypeStruct((8, slots), jnp.int32),
            jax.ShapeDtypeStruct((chunks // 2 * sub + 8, LANES), jnp.float32),
            jax.ShapeDtypeStruct((8, LANES), jnp.float32),
        ),
        in_specs=[
            pl.BlockSpec(memory_space=pl.ANY),
            pl.BlockSpec(memory_space=pl.ANY),
        ],
        out_specs=(
            pl.BlockSpec(memory_space=pl.ANY),
            pl.BlockSpec(memory_space=pl.ANY),
            pl.BlockSpec(memory_space=pltpu.SMEM),
            pl.BlockSpec(memory_space=pltpu.VMEM),
            pl.BlockSpec(memory_space=pltpu.VMEM),
        ),
        scratch_shapes=[
            pltpu.VMEM((8, slots // 8, chunks * blk, LANES), jnp.bfloat16),
            pltpu.VMEM((slots, META, LANES), jnp.bfloat16),
            pltpu.VMEM((lists, width), jnp.float32),
            pltpu.VMEM((chunks + 1, rows + GROUP + blk, LANES), jnp.float32),
            pltpu.VMEM((groups, lists, GROUP), jnp.bfloat16),
            pltpu.VMEM((groups, width, GROUP), jnp.bfloat16),
            pltpu.VMEM((LANES, LANES), jnp.float32),
            pltpu.VMEM((8, slots), jnp.int32),
            pltpu.VMEM((lists, width), jnp.float32),
            pltpu.VMEM((lists, LANES), jnp.float32),
            pltpu.VMEM((width, 2 * lists), jnp.bfloat16),
            pltpu.VMEM((width // (2 * LANES), 2 * LANES, 2 * LANES), jnp.float32),
            pltpu.VMEM((lists, width), jnp.float32),
            pltpu.SemaphoreType.DMA((10,)),
            pltpu.SemaphoreType.DMA((groups,)),
        ],
        compiler_params=pltpu.CompilerParams(vmem_limit_bytes=VMEM),
        name="update_lists",
    )(recv, old)


def error_kernel(sub, part, pieces, blk, place_ref, resid_ref, book_ref, before_ref, error_ref, *rest):
    slot_ref = rest[0] if part == pieces - 1 else None
    held, sems = rest[-2:]
    subspaces = book_ref.shape[0]
    slots = place_ref.shape[1]
    width = subspaces * sub
    used = place_ref[0, slots - 1] + place_ref[1, slots - 1]
    groups = (used + GROUP - 1) // GROUP
    first, last = part * groups // pieces, (part + 1) * groups // pieces
    error_ref[...] = before_ref[...]

    def fetch(g):
        at = lax.rem(g, 2)
        return pltpu.make_async_copy(resid_ref.at[g], held.at[at], sems.at[at])

    @pl.when(first < last)
    def _():
        fetch(first).start()

    ones = jnp.ones((AUG, GROUP), jnp.bfloat16)

    def visit(g, carry):
        @pl.when(g + 1 < last)
        def _():
            fetch(g + 1).start()

        fetch(g).wait()
        at = lax.rem(g, 2)
        norm = jnp.zeros((8, GROUP), jnp.float32)
        least = jnp.zeros((1, GROUP), jnp.float32)
        for m in range(subspaces):
            piece = held[at, m * sub : (m + 1) * sub, :]
            long = piece.astype(jnp.float32)
            square = long * long
            for k in range(sub // 8):
                norm = norm + square[k * 8 : (k + 1) * 8]
            distance = jnp.dot(
                book_ref[m],
                jnp.concatenate([piece, ones], axis=0),
                preferred_element_type=jnp.float32,
            )
            least = least + jnp.min(distance, axis=0, keepdims=True)
        error = (least + jnp.sum(norm, axis=0, keepdims=True)) / width
        for k in range(GROUP // LANES):
            error_ref[pl.ds(g * (GROUP // LANES) + k, 1), :] = error[:, k * LANES : (k + 1) * LANES]
        return carry

    lax.fori_loop(first, last, visit, 0)

    if slot_ref is not None:
        lane = lax.broadcasted_iota(jnp.int32, (1, LANES), 1)
        for s in range(slots):
            start = place_ref[0, s]
            line = start // LANES
            shift = lax.rem(start, LANES)
            window = jnp.where(
                lane >= shift, error_ref[pl.ds(line, 1), :], error_ref[pl.ds(line + 1, 1), :]
            )
            window = pltpu.roll(window, lax.rem(LANES - shift, LANES), 1)
            window = jnp.where(lane < place_ref[1, s], window, 0.0)
            slot_ref[s : s + 1, :] = window[:, 0:blk]


def row_errors(place, resid, book, before, sub, blk, part, pieces):
    groups, width, _ = resid.shape
    subspaces, codes, depth = book.shape
    slots = place.shape[1]
    lines = slots * blk // LANES + 8
    out = [jax.ShapeDtypeStruct((lines, LANES), jnp.float32)]
    if part == pieces - 1:
        out.append(jax.ShapeDtypeStruct((slots, blk), jnp.float32))
    return pl.pallas_call(
        functools.partial(error_kernel, sub, part, pieces, blk),
        out_shape=tuple(out),
        in_specs=[
            pl.BlockSpec(memory_space=pltpu.SMEM),
            pl.BlockSpec(memory_space=pl.ANY),
            pl.BlockSpec(memory_space=pltpu.VMEM),
            pl.BlockSpec(memory_space=pltpu.VMEM),
        ],
        out_specs=tuple(pl.BlockSpec(memory_space=pltpu.VMEM) for _ in out),
        scratch_shapes=[
            pltpu.VMEM((2, width, GROUP), jnp.bfloat16),
            pltpu.SemaphoreType.DMA((2,)),
        ],
        compiler_params=pltpu.CompilerParams(vmem_limit_bytes=VMEM // 2),
        cost_estimate=pl.CostEstimate(
            flops=2 * 256 * codes * subspaces * GROUP * 3,
            bytes_accessed=width * GROUP * 2 * 3,
            transcendentals=0,
        ),
        name="row_errors",
    )(place, resid, book, before)


def unpack_kernel(one_ref, two_ref, three_ref, four_ref, total_ref, out_ref):
    sub = out_ref.shape[1]
    across = LANES // sub
    half = out_ref.shape[0] // across // 2
    packed = (one_ref[...] + two_ref[...]) + (three_ref[...] + four_ref[...])
    share = 1.0 / total_ref[0:1, 0:1]
    row = lax.broadcasted_iota(jnp.int32, (sub, sub), 0)
    lane = lax.broadcasted_iota(jnp.int32, (sub, sub), 1)
    for q in range(half):
        square = packed[q * sub : (q + 1) * sub]
        turned = square.T
        for a in range(across):
            at = slice(a * sub, (a + 1) * sub)
            here, flip = square[:, at], turned[at]
            diagonal = packed[half * sub + q : half * sub + q + 1, at]
            out_ref[q * across + a] = jnp.where(row <= lane, here, flip) * share
            other = jnp.where(row > lane, here, jnp.where(row < lane, flip, diagonal))
            out_ref[(half + q) * across + a] = other * share


def unpack_moments(terms, total, subspaces, sub):
    return pl.pallas_call(
        unpack_kernel,
        out_shape=jax.ShapeDtypeStruct((subspaces, sub, sub), jnp.float32),
        name="unpack_moments",
    )(*terms, total)


def extended_book(codebook):
    values = codebook.astype(jnp.float32)
    rest = jnp.sum(jnp.square(values), axis=1)
    parts = []
    for _ in range(3):
        part = lax.reduce_precision(rest, 8, 7)
        parts.append(part)
        rest = rest - part
    parts = jnp.stack(parts, axis=2)
    parts = jnp.pad(parts, ((0, 0), (0, 0), (0, AUG - 3)))
    return jnp.concatenate([-2.0 * values.transpose(0, 2, 1), parts], axis=2).astype(jnp.bfloat16)


def body(vectors, row_list, block_owner, block_fill, old_centroids, codebook):
    devices = lax.axis_size("dev")
    blk = row_list.shape[0] // block_owner.shape[0]
    sub = codebook.shape[1]
    width = vectors.shape[1]
    book = extended_book(codebook)
    send = build_send(vectors, row_list, block_owner, block_fill, devices)
    recv = lax.all_to_all(send, "dev", split_axis=0, concat_axis=0, tiled=True)
    centroids, resid, place, packed, total = update_lists(recv, old_centroids, blk, sub)
    pieces = 4
    errors = jnp.zeros((devices * blk // LANES + 8, LANES), jnp.float32)
    slot_error = None
    for part in range(pieces):
        out = row_errors(place, resid, book, errors, sub, blk, part, pieces)
        errors, slot_error = out[0], out[-1]

    def partner(step):
        return lax.ppermute(packed, "dev", [(i, i ^ step) for i in range(devices)])

    packed = packed + partner(1)
    stride = 2
    while True:
        terms = (packed, partner(stride), partner(2 * stride), partner(3 * stride))
        stride *= 4
        if stride >= devices:
            break
        packed = (terms[0] + terms[1]) + (terms[2] + terms[3])
    moments = unpack_moments(terms, total, codebook.shape[0], sub)
    return centroids, slot_error, moments


def solution(mesh):
    return jax.shard_map(
        body,
        mesh=mesh,
        in_specs=(P("dev", None), P("dev"), P("dev"), P("dev"), P("dev", None), P()),
        out_specs=(P("dev", None), P("dev", None), P()),
        check_vma=False,
    )
```

```python
import functools

import jax
import jax.numpy as jnp
from jax import lax
from jax.experimental import pallas as pl
from jax.experimental.pallas import tpu as pltpu
from jax.sharding import PartitionSpec as P

LANES = 128
META = 8
AUG = 16
GROUP = 256
VMEM = 42 * 1024 * 1024
LARGE_VMEM = 56 * 1024 * 1024
SMALL_VMEM = 10 * 1024 * 1024
BOUNDS = ((0, 0), (1, 8), (4, 4), (7, 4), (9, 0))


def send_kernel(blk, owner_ref, fill_ref, vec_ref, list_ref, send_ref, held, tiles, meta, sems):
    blocks = owner_ref.shape[0]
    width = vec_ref.shape[1]
    chunks = width // LANES
    span = LANES // blk
    me = lax.axis_index("dev")
    place = lax.rem(me, span)
    stages = held.shape[0]
    some = blocks // stages
    loads = [
        pltpu.make_async_copy(
            vec_ref.at[pl.ds(c * some * blk, some * blk), :], held.at[c], sems.at[blocks + 1 + c]
        )
        for c in range(stages)
    ]
    for load in loads:
        load.start()
    total = functools.reduce(lambda a, b: a + b, [fill_ref[b] for b in range(blocks)])
    rows = lax.broadcasted_iota(jnp.int32, (META, LANES), 0)
    lane = lax.broadcasted_iota(jnp.int32, (1, LANES), 1)
    base = jnp.where(rows == 3, total >> 8, jnp.where(rows == 4, total & 255, 0))
    meta[...] = jnp.broadcast_to(base.astype(jnp.float32).astype(jnp.bfloat16)[None], meta.shape)
    for b in range(blocks):
        line = list_ref[b // span : b // span + 1, :] + 1
        line = pltpu.roll(line, lax.rem(place + span - b % span, span) * blk, 1)
        kept = (lane // blk == place) & (lax.rem(lane, blk) < fill_ref[b])
        line = jnp.broadcast_to(jnp.where(kept, line, 0), (META, LANES))
        count = jnp.broadcast_to(jnp.where(lane == me, fill_ref[b], 0), (META, LANES))
        tile = jnp.where(
            rows == 0, line & 255, jnp.where(rows == 1, line >> 8, jnp.where(rows == 2, count, base))
        )
        meta[owner_ref[b]] = tile.astype(jnp.float32).astype(jnp.bfloat16)
    last = pltpu.make_async_copy(
        meta, send_ref.at[:, pl.ds(chunks * blk, META), :], sems.at[blocks]
    )
    last.start()
    copies = []
    for c in range(stages):
        loads[c].wait()
        for b in range(c * some, (c + 1) * some):
            at = slice((b - c * some) * blk, (b - c * some + 1) * blk)
            for j in range(chunks):
                tiles[b, j * blk : (j + 1) * blk, :] = held[c, at, j * LANES : (j + 1) * LANES]
            copy = pltpu.make_async_copy(
                tiles.at[b], send_ref.at[owner_ref[b], pl.ds(0, chunks * blk), :], sems.at[b]
            )
            copy.start()
            copies.append(copy)
    for copy in copies:
        copy.wait()
    last.wait()


def build_send(vectors, row_list, block_owner, block_fill, devices):
    rows, width = vectors.shape
    blocks = block_owner.shape[0]
    blk = rows // blocks
    height = width // LANES * blk
    return pl.pallas_call(
        functools.partial(send_kernel, blk),
        out_shape=jax.ShapeDtypeStruct((devices, height + META, LANES), jnp.bfloat16),
        in_specs=[
            pl.BlockSpec(memory_space=pltpu.SMEM),
            pl.BlockSpec(memory_space=pltpu.SMEM),
            pl.BlockSpec(memory_space=pl.ANY),
            pl.BlockSpec(memory_space=pltpu.VMEM),
        ],
        out_specs=pl.BlockSpec(memory_space=pl.ANY),
        scratch_shapes=[
            pltpu.VMEM((4, rows // 4, width), jnp.bfloat16),
            pltpu.VMEM((blocks, height, LANES), jnp.bfloat16),
            pltpu.VMEM((devices, META, LANES), jnp.bfloat16),
            pltpu.SemaphoreType.DMA((blocks + 5,)),
        ],
        compiler_params=pltpu.CompilerParams(vmem_limit_bytes=LARGE_VMEM),
        name="build_send",
    )(block_owner, block_fill, vectors, row_list.reshape(rows // LANES, LANES))


def update_kernel(
    blk, recv_ref, old_ref, cent_ref, resid_ref, where_ref, packed_ref, total_ref,
    blocks, info, old, dense, hot, turned, column, place_ref, sums, counts, parts, gram, sems, out_sems,
):
    slots, height, _ = recv_ref.shape
    lists, width = old_ref.shape
    chunks = width // LANES
    span = LANES // blk
    some = slots // blocks.shape[0]
    rows = slots * blk

    notes = pltpu.make_async_copy(recv_ref.at[:, pl.ds(chunks * blk, META), :], info, sems.at[0])
    notes.start()

    def fetch(c):
        return pltpu.make_async_copy(
            recv_ref.at[pl.ds(c * some, some), pl.ds(0, chunks * blk), :], blocks.at[c], sems.at[1 + c]
        )

    for c in range(blocks.shape[0]):
        fetch(c).start()

    own = pltpu.make_async_copy(old_ref, old, sems.at[1 + blocks.shape[0]])
    own.start()
    notes.wait()
    lines, seen = [], jnp.zeros((META, LANES), jnp.float32)
    for q in range(slots // span):
        note = info[q * span].astype(jnp.float32)
        for s in range(1, span):
            note = note + info[q * span + s].astype(jnp.float32)
        lines.append(note[0:1] + 256.0 * note[1:2])
        seen = seen + note
    fill = jnp.broadcast_to(seen[2:3], (8, LANES))
    before = lax.broadcasted_iota(jnp.int32, (slots, slots), 0)
    after = lax.broadcasted_iota(jnp.int32, (slots, slots), 1)
    start = jnp.dot(
        fill.astype(jnp.bfloat16),
        jnp.where(before < after, 1.0, 0.0).astype(jnp.bfloat16),
        preferred_element_type=jnp.float32,
    )
    which = lax.broadcasted_iota(jnp.int32, (8, slots), 0)
    where_ref[...] = jnp.where(which == 0, start, fill).astype(jnp.int32)
    mover = pltpu.make_async_copy(where_ref, place_ref, sems.at[0])
    mover.start()
    total_ref[...] = jnp.broadcast_to(seen[4:5] + 256.0 * seen[3:4], total_ref.shape)
    lines.append(jnp.zeros((LANES - len(lines), LANES), jnp.float32))
    column[...] = jnp.concatenate(lines, axis=0).T
    sums[...] = jnp.zeros_like(sums)
    counts[...] = jnp.zeros_like(counts)
    gram[...] = jnp.zeros_like(gram)
    mover.wait()

    lane = lax.broadcasted_iota(jnp.int32, (blk, LANES), 1)

    def pack(c, carry):
        fetch(c).wait()
        for s in range(some):
            at = pl.ds(place_ref[0, c * some + s], blk)
            for j in range(chunks):
                dense[j, at, :] = blocks[c, s, j * blk : (j + 1) * blk, :].astype(jnp.float32)
            ids = column[(s % span) * blk : (s % span + 1) * blk, :]
            dense[chunks, at, :] = jnp.where(lane == c * (some // span) + s // span, ids, 0.0)
        return carry

    lax.fori_loop(0, blocks.shape[0], pack, 0)
    used = place_ref[0, slots - 1] + place_ref[1, slots - 1]
    for j in range(chunks + 1):
        dense[j, pl.ds(used, GROUP + blk), :] = jnp.zeros((GROUP + blk, LANES), jnp.float32)
    groups = (used + GROUP - 1) // GROUP

    def gather(g, carry):
        at = pl.ds(pl.multiple_of(g * GROUP, GROUP), GROUP)
        code = jnp.sum(dense[chunks, at, :].T, axis=0, keepdims=True)
        ids = lax.broadcasted_iota(jnp.int32, (lists, GROUP), 0).astype(jnp.float32) + 1.0
        match = jnp.where(ids == code, 1.0, 0.0)
        chosen = match.astype(jnp.bfloat16)
        hot[g] = chosen
        part = match[:, 0:LANES]
        for k in range(1, GROUP // LANES):
            part = part + match[:, k * LANES : (k + 1) * LANES]
        counts[...] += part
        pieces = []
        for j in range(chunks):
            piece = dense[j, at, :].astype(jnp.bfloat16)
            turned[g, j * LANES : (j + 1) * LANES, :] = piece.T
            pieces.append(piece)
        sums[...] += jnp.dot(
            chosen, jnp.concatenate(pieces, axis=1), preferred_element_type=jnp.float32
        )
        return carry

    lax.fori_loop(0, groups, gather, 0)

    count = jnp.sum(counts[...], axis=1, keepdims=True) + 1.0
    own.wait()
    cent = (sums[...] + old[...]) / count
    sums[...] = cent
    write = pltpu.make_async_copy(sums, cent_ref, sems.at[0])
    write.start()
    flipped = cent.T
    head = flipped.astype(jnp.bfloat16)
    parts[:, 0:lists] = head
    parts[:, lists : 2 * lists] = (flipped - head.astype(jnp.float32)).astype(jnp.bfloat16)

    wide = 2 * LANES
    lane = lax.broadcasted_iota(jnp.int32, (1, GROUP), 1)

    def leave(g):
        return pltpu.make_async_copy(turned.at[g], resid_ref.at[g], out_sems.at[g])

    def encode(g, carry):
        chosen = hot[g]
        weight = jnp.where(lane < used - g * GROUP, 1.0, 0.0)
        both = jnp.concatenate([chosen, chosen], axis=0)
        resids = []
        for j in range(width // wide):
            at = slice(j * wide, (j + 1) * wide)
            picked = jnp.dot(parts[at], both, preferred_element_type=jnp.float32)
            resids.append(((turned[g, at].astype(jnp.float32) - picked) * weight).astype(jnp.bfloat16))
        for j in range(width // wide):
            turned[g, j * wide : (j + 1) * wide] = resids[j]
        squares = [
            lax.dot_general(r, r, (((1,), (1,)), ((), ())), preferred_element_type=jnp.float32)
            for r in resids
        ]
        for j in range(width // wide):
            gram[j] += squares[j]
        leave(g).start()
        return carry

    lax.fori_loop(0, groups, encode, 0)

    sub = (packed_ref.shape[0] - 8) // (chunks // 2)
    across = LANES // sub
    row = lax.broadcasted_iota(jnp.int32, (sub, LANES), 0)
    lane = lax.broadcasted_iota(jnp.int32, (sub, LANES), 1)
    squares = []
    for q in range(chunks):
        half = slice((q % 2) * LANES, (q % 2 + 1) * LANES)
        square = jnp.zeros((sub, LANES), jnp.float32)
        for a in range(across):
            top = ((q % 2) * across + a) * sub
            square = jnp.where(lane // sub == a, gram[q // 2, top : top + sub, half], square)
        squares.append(square)
    half = chunks // 2
    diagonals = []
    for q in range(half):
        packed_ref[q * sub : (q + 1) * sub, :] = jnp.where(
            row <= lane % sub, squares[q], squares[half + q]
        )
        diagonals.append(
            jnp.sum(jnp.where(row == lane % sub, squares[half + q], 0.0), axis=0, keepdims=True)
        )
    diagonals.append(jnp.zeros((8 - half, LANES), jnp.float32))
    packed_ref[half * sub :, :] = jnp.concatenate(diagonals, axis=0)

    def finish(g, carry):
        leave(g).wait()
        return carry

    lax.fori_loop(0, groups, finish, 0)
    write.wait()


def update_lists(recv, old, blk, sub):
    slots, height, _ = recv.shape
    lists, width = old.shape
    rows = slots * blk
    groups = rows // GROUP
    chunks = width // LANES
    return pl.pallas_call(
        functools.partial(update_kernel, blk),
        out_shape=(
            jax.ShapeDtypeStruct((lists, width), jnp.float32),
            jax.ShapeDtypeStruct((groups, width, GROUP), jnp.bfloat16),
            jax.ShapeDtypeStruct((8, slots), jnp.int32),
            jax.ShapeDtypeStruct((chunks // 2 * sub + 8, LANES), jnp.float32),
            jax.ShapeDtypeStruct((8, LANES), jnp.float32),
        ),
        in_specs=[
            pl.BlockSpec(memory_space=pl.ANY),
            pl.BlockSpec(memory_space=pl.ANY),
        ],
        out_specs=(
            pl.BlockSpec(memory_space=pl.ANY),
            pl.BlockSpec(memory_space=pl.ANY),
            pl.BlockSpec(memory_space=pltpu.VMEM),
            pl.BlockSpec(memory_space=pltpu.VMEM),
            pl.BlockSpec(memory_space=pltpu.VMEM),
        ),
        scratch_shapes=[
            pltpu.VMEM((8, slots // 8, chunks * blk, LANES), jnp.bfloat16),
            pltpu.VMEM((slots, META, LANES), jnp.bfloat16),
            pltpu.VMEM((lists, width), jnp.float32),
            pltpu.VMEM((chunks + 1, rows + GROUP + blk, LANES), jnp.float32),
            pltpu.VMEM((groups, lists, GROUP), jnp.bfloat16),
            pltpu.VMEM((groups, width, GROUP), jnp.bfloat16),
            pltpu.VMEM((LANES, LANES), jnp.float32),
            pltpu.SMEM((8, slots), jnp.int32),
            pltpu.VMEM((lists, width), jnp.float32),
            pltpu.VMEM((lists, LANES), jnp.float32),
            pltpu.VMEM((width, 2 * lists), jnp.bfloat16),
            pltpu.VMEM((width // (2 * LANES), 2 * LANES, 2 * LANES), jnp.float32),
            pltpu.SemaphoreType.DMA((10,)),
            pltpu.SemaphoreType.DMA((groups,)),
        ],
        compiler_params=pltpu.CompilerParams(vmem_limit_bytes=VMEM),
        name="update_lists",
    )(recv, old)


def error_kernel(sub, part, blk, place_ref, resid_ref, book_ref, *rest):
    before_ref, error_ref = rest[:2] if part else (None, rest[0])
    slot_ref, lines = rest[2:4] if part == len(BOUNDS) - 2 else (None, None)
    subspaces = book_ref.shape[0]
    slots = place_ref.shape[1]
    width = subspaces * sub
    used = place_ref[0, slots - 1] + place_ref[1, slots - 1]
    groups = (used + GROUP - 1) // GROUP
    first, last = (
        (groups * top + rest) // BOUNDS[-1][0] for top, rest in (BOUNDS[part], BOUNDS[part + 1])
    )
    error_ref[...] = before_ref[...] if part else jnp.zeros_like(error_ref)

    ones = jnp.ones((AUG, GROUP), jnp.bfloat16)

    def visit(g, carry):
        norm = jnp.zeros((8, GROUP), jnp.float32)
        least = jnp.zeros((1, GROUP), jnp.float32)
        for m in range(subspaces):
            piece = resid_ref[g, m * sub : (m + 1) * sub, :]
            long = piece.astype(jnp.float32)
            square = long * long
            for k in range(sub // 8):
                norm = norm + square[k * 8 : (k + 1) * 8]
            distance = jnp.dot(
                book_ref[m],
                jnp.concatenate([piece, ones], axis=0),
                preferred_element_type=jnp.float32,
            )
            least = least + jnp.min(distance, axis=0, keepdims=True)
        error = (least + jnp.sum(norm, axis=0, keepdims=True)) / width
        for k in range(GROUP // LANES):
            error_ref[pl.ds(g * (GROUP // LANES) + k, 1), :] = error[:, k * LANES : (k + 1) * LANES]
        return carry

    lax.fori_loop(first, last, visit, 0)

    if slot_ref is not None:
        lane = lax.broadcasted_iota(jnp.int32, (1, LANES), 1)
        for s in range(slots):
            start = place_ref[0, s]
            line = start // LANES
            shift = lax.rem(start, LANES)
            window = jnp.where(
                lane >= shift, error_ref[pl.ds(line, 1), :], error_ref[pl.ds(line + 1, 1), :]
            )
            window = pltpu.roll(window, lax.rem(LANES - shift, LANES), 1)
            window = jnp.where(lane < place_ref[1, s], window, 0.0)
            lines[s : s + 1, :] = window
        slot_ref[...] = lines[...].T[0:blk]


def row_errors(place, resid, book, before, sub, blk, part):
    groups, width, _ = resid.shape
    subspaces, codes, depth = book.shape
    slots = place.shape[1]
    vmem = pl.BlockSpec(memory_space=pltpu.VMEM)
    out = [jax.ShapeDtypeStruct((slots * blk // LANES + 8, LANES), jnp.float32)]
    scratch = []
    if part == len(BOUNDS) - 2:
        out.append(jax.ShapeDtypeStruct((blk, slots), jnp.float32))
        scratch.append(pltpu.VMEM((slots, LANES), jnp.float32))
    operands = [place, resid, book] + ([before] if part else [])
    return pl.pallas_call(
        functools.partial(error_kernel, sub, part, blk),
        out_shape=tuple(out),
        in_specs=[
            pl.BlockSpec(memory_space=pltpu.SMEM),
            vmem,
            vmem,
            vmem,
        ][: len(operands)],
        out_specs=tuple(vmem for _ in out),
        scratch_shapes=scratch,
        compiler_params=pltpu.CompilerParams(vmem_limit_bytes=SMALL_VMEM),
        cost_estimate=pl.CostEstimate(
            flops=2 * 256 * codes * subspaces * GROUP * 3,
            bytes_accessed=width * GROUP * 2 * 3,
            transcendentals=0,
        ),
        name="row_errors",
    )(*operands)


def unpack_kernel(one_ref, two_ref, three_ref, four_ref, total_ref, out_ref):
    sub = out_ref.shape[1]
    across = LANES // sub
    half = out_ref.shape[0] // across // 2
    packed = (one_ref[...] + two_ref[...]) + (three_ref[...] + four_ref[...])
    share = 1.0 / total_ref[0:1, 0:1]
    row = lax.broadcasted_iota(jnp.int32, (sub, sub), 0)
    lane = lax.broadcasted_iota(jnp.int32, (sub, sub), 1)
    for q in range(half):
        square = packed[q * sub : (q + 1) * sub]
        turned = square.T
        for a in range(across):
            at = slice(a * sub, (a + 1) * sub)
            here, flip = square[:, at], turned[at]
            diagonal = packed[half * sub + q : half * sub + q + 1, at]
            out_ref[q * across + a] = jnp.where(row <= lane, here, flip) * share
            other = jnp.where(row > lane, here, jnp.where(row < lane, flip, diagonal))
            out_ref[(half + q) * across + a] = other * share


def unpack_moments(terms, total, subspaces, sub):
    return pl.pallas_call(
        unpack_kernel,
        out_shape=jax.ShapeDtypeStruct((subspaces, sub, sub), jnp.float32),
        compiler_params=pltpu.CompilerParams(vmem_limit_bytes=SMALL_VMEM),
        name="unpack_moments",
    )(*terms, total)


def extended_book(codebook):
    values = codebook.astype(jnp.float32)
    rest = jnp.sum(jnp.square(values), axis=1)
    parts = []
    for _ in range(3):
        part = lax.reduce_precision(rest, 8, 7)
        parts.append(part)
        rest = rest - part
    parts = jnp.stack(parts, axis=2)
    parts = jnp.pad(parts, ((0, 0), (0, 0), (0, AUG - 3)))
    return jnp.concatenate([-2.0 * values.transpose(0, 2, 1), parts], axis=2).astype(jnp.bfloat16)


def body(vectors, row_list, block_owner, block_fill, old_centroids, codebook):
    devices = lax.axis_size("dev")
    blk = row_list.shape[0] // block_owner.shape[0]
    sub = codebook.shape[1]
    width = vectors.shape[1]
    book = extended_book(codebook)
    send = build_send(vectors, row_list, block_owner, block_fill, devices)
    recv = lax.all_to_all(send, "dev", split_axis=0, concat_axis=0, tiled=True)
    centroids, resid, place, packed, total = update_lists(recv, old_centroids, blk, sub)
    errors, slot_error = None, None
    for part in range(len(BOUNDS) - 1):
        out = row_errors(place, resid, book, errors, sub, blk, part)
        errors, slot_error = out[0], out[-1]

    def partner(step):
        return lax.ppermute(packed, "dev", [(i, i ^ step) for i in range(devices)])

    packed = packed + partner(1)
    stride = 2
    while True:
        terms = (packed, partner(stride), partner(2 * stride), partner(3 * stride))
        stride *= 4
        if stride >= devices:
            break
        packed = (terms[0] + terms[1]) + (terms[2] + terms[3])
    moments = unpack_moments(terms, total, codebook.shape[0], sub)
    return centroids, slot_error.T, moments


def solution(mesh):
    return jax.shard_map(
        body,
        mesh=mesh,
        in_specs=(P("dev", None), P("dev"), P("dev"), P("dev"), P("dev", None), P()),
        out_specs=(P("dev", None), P("dev", None), P()),
        check_vma=False,
    )
```

```python
import functools

import jax
import jax.numpy as jnp
from jax import lax
from jax.experimental import pallas as pl
from jax.experimental.pallas import tpu as pltpu
from jax.sharding import PartitionSpec as P

LANES = 128
META = 8
AUG = 16
GROUP = 256
VMEM = 37 * 1024 * 1024
LARGE_VMEM = 56 * 1024 * 1024
SMALL_VMEM = 10 * 1024 * 1024
BOUNDS = ((0, 0), (1, 8), (4, 4), (7, 4), (9, 0))


def send_kernel(blk, owner_ref, fill_ref, vec_ref, list_ref, send_ref, held, tiles, meta, sems):
    blocks = owner_ref.shape[0]
    width = vec_ref.shape[1]
    chunks = width // LANES
    span = LANES // blk
    me = lax.axis_index("dev")
    place = lax.rem(me, span)
    stages = held.shape[0]
    some = blocks // stages
    loads = [
        pltpu.make_async_copy(
            vec_ref.at[pl.ds(c * some * blk, some * blk), :], held.at[c], sems.at[blocks + 1 + c]
        )
        for c in range(stages)
    ]
    for load in loads:
        load.start()
    total = functools.reduce(lambda a, b: a + b, [fill_ref[b] for b in range(blocks)])
    rows = lax.broadcasted_iota(jnp.int32, (META, LANES), 0)
    lane = lax.broadcasted_iota(jnp.int32, (1, LANES), 1)
    base = jnp.where(rows == 3, total >> 8, jnp.where(rows == 4, total & 255, 0))
    meta[...] = jnp.broadcast_to(base.astype(jnp.float32).astype(jnp.bfloat16)[None], meta.shape)
    for b in range(blocks):
        line = list_ref[b // span : b // span + 1, :] + 1
        line = pltpu.roll(line, lax.rem(place + span - b % span, span) * blk, 1)
        kept = (lane // blk == place) & (lax.rem(lane, blk) < fill_ref[b])
        line = jnp.broadcast_to(jnp.where(kept, line, 0), (META, LANES))
        count = jnp.broadcast_to(jnp.where(lane == me, fill_ref[b], 0), (META, LANES))
        tile = jnp.where(
            rows == 0, line & 255, jnp.where(rows == 1, line >> 8, jnp.where(rows == 2, count, base))
        )
        meta[owner_ref[b]] = tile.astype(jnp.float32).astype(jnp.bfloat16)
    last = pltpu.make_async_copy(
        meta, send_ref.at[:, pl.ds(chunks * blk, META), :], sems.at[blocks]
    )
    last.start()
    copies = []
    for c in range(stages):
        loads[c].wait()
        for b in range(c * some, (c + 1) * some):
            at = slice((b - c * some) * blk, (b - c * some + 1) * blk)
            for j in range(chunks):
                tiles[b, j * blk : (j + 1) * blk, :] = held[c, at, j * LANES : (j + 1) * LANES]
            copy = pltpu.make_async_copy(
                tiles.at[b], send_ref.at[owner_ref[b], pl.ds(0, chunks * blk), :], sems.at[b]
            )
            copy.start()
            copies.append(copy)
    for copy in copies:
        copy.wait()
    last.wait()


def build_send(vectors, row_list, block_owner, block_fill, devices):
    rows, width = vectors.shape
    blocks = block_owner.shape[0]
    blk = rows // blocks
    height = width // LANES * blk
    return pl.pallas_call(
        functools.partial(send_kernel, blk),
        out_shape=jax.ShapeDtypeStruct((devices, height + META, LANES), jnp.bfloat16),
        in_specs=[
            pl.BlockSpec(memory_space=pltpu.SMEM),
            pl.BlockSpec(memory_space=pltpu.SMEM),
            pl.BlockSpec(memory_space=pl.ANY),
            pl.BlockSpec(memory_space=pltpu.VMEM),
        ],
        out_specs=pl.BlockSpec(memory_space=pl.ANY),
        scratch_shapes=[
            pltpu.VMEM((4, rows // 4, width), jnp.bfloat16),
            pltpu.VMEM((blocks, height, LANES), jnp.bfloat16),
            pltpu.VMEM((devices, META, LANES), jnp.bfloat16),
            pltpu.SemaphoreType.DMA((blocks + 5,)),
        ],
        compiler_params=pltpu.CompilerParams(vmem_limit_bytes=LARGE_VMEM),
        name="build_send",
    )(block_owner, block_fill, vectors, row_list.reshape(rows // LANES, LANES))


def update_kernel(
    blk, recv_ref, old_ref, cent_ref, turned, where_ref, packed_ref, total_ref,
    blocks, info, old, dense, hot, values, column, place_ref, sums, counts, parts, gram, sems,
):
    slots, height, _ = recv_ref.shape
    lists, width = old_ref.shape
    chunks = width // LANES
    span = LANES // blk
    some = slots // blocks.shape[0]
    rows = slots * blk

    notes = pltpu.make_async_copy(recv_ref.at[:, pl.ds(chunks * blk, META), :], info, sems.at[0])
    notes.start()

    def fetch(c):
        return pltpu.make_async_copy(
            recv_ref.at[pl.ds(c * some, some), pl.ds(0, chunks * blk), :], blocks.at[c], sems.at[1 + c]
        )

    for c in range(blocks.shape[0]):
        fetch(c).start()

    own = pltpu.make_async_copy(old_ref, old, sems.at[1 + blocks.shape[0]])
    own.start()
    notes.wait()
    lines, seen = [], jnp.zeros((META, LANES), jnp.float32)
    for q in range(slots // span):
        note = info[q * span].astype(jnp.float32)
        for s in range(1, span):
            note = note + info[q * span + s].astype(jnp.float32)
        lines.append(note[0:1] + 256.0 * note[1:2])
        seen = seen + note
    fill = jnp.broadcast_to(seen[2:3], (8, LANES))
    before = lax.broadcasted_iota(jnp.int32, (slots, slots), 0)
    after = lax.broadcasted_iota(jnp.int32, (slots, slots), 1)
    start = jnp.dot(
        fill.astype(jnp.bfloat16),
        jnp.where(before < after, 1.0, 0.0).astype(jnp.bfloat16),
        preferred_element_type=jnp.float32,
    )
    which = lax.broadcasted_iota(jnp.int32, (8, slots), 0)
    where_ref[...] = jnp.where(which == 0, start, fill).astype(jnp.int32)
    mover = pltpu.make_async_copy(where_ref, place_ref, sems.at[0])
    mover.start()
    total_ref[...] = jnp.broadcast_to(seen[4:5] + 256.0 * seen[3:4], total_ref.shape)
    lines.append(jnp.zeros((LANES - len(lines), LANES), jnp.float32))
    column[...] = jnp.concatenate(lines, axis=0).T
    sums[...] = jnp.zeros_like(sums)
    counts[...] = jnp.zeros_like(counts)
    gram[...] = jnp.zeros_like(gram)
    mover.wait()

    lane = lax.broadcasted_iota(jnp.int32, (blk, LANES), 1)

    def pack(c, carry):
        fetch(c).wait()
        for s in range(some):
            at = pl.ds(place_ref[0, c * some + s], blk)
            for j in range(chunks):
                dense[j, at, :] = blocks[c, s, j * blk : (j + 1) * blk, :].astype(jnp.float32)
            ids = column[(s % span) * blk : (s % span + 1) * blk, :]
            dense[chunks, at, :] = jnp.where(lane == c * (some // span) + s // span, ids, 0.0)
        return carry

    lax.fori_loop(0, blocks.shape[0], pack, 0)
    used = place_ref[0, slots - 1] + place_ref[1, slots - 1]
    for j in range(chunks + 1):
        dense[j, pl.ds(used, GROUP + blk), :] = jnp.zeros((GROUP + blk, LANES), jnp.float32)
    groups = jnp.maximum((used + GROUP - 1) // GROUP, 1)

    def prepare(g):
        at = pl.ds(pl.multiple_of(g * GROUP, GROUP), GROUP)
        code = jnp.sum(dense[chunks, at, :].T, axis=0, keepdims=True)
        ids = lax.broadcasted_iota(jnp.int32, (lists, GROUP), 0).astype(jnp.float32) + 1.0
        hot[g] = jnp.where(ids == code, 1.0, 0.0).astype(jnp.bfloat16)
        for j in range(chunks):
            piece = dense[j, at, :].astype(jnp.bfloat16)
            turned[g, j * LANES : (j + 1) * LANES, :] = piece.T
            values[g & 1, :, j * LANES : (j + 1) * LANES] = piece

    prepare(0)

    def gather(g, carry):
        chosen = hot[g]
        added = jnp.dot(chosen, values[g & 1], preferred_element_type=jnp.float32)
        part = chosen[:, 0:LANES].astype(jnp.float32)
        for k in range(1, GROUP // LANES):
            part = part + chosen[:, k * LANES : (k + 1) * LANES].astype(jnp.float32)
        prepare(g + 1)
        sums[...] += added
        counts[...] += part
        return carry

    lax.fori_loop(0, groups, gather, 0)

    count = jnp.sum(counts[...], axis=1, keepdims=True) + 1.0
    own.wait()
    cent = (sums[...] + old[...]) / count
    sums[...] = cent
    write = pltpu.make_async_copy(sums, cent_ref, sems.at[0])
    write.start()
    flipped = cent.T
    head = flipped.astype(jnp.bfloat16)
    parts[:, 0:lists] = head
    parts[:, lists : 2 * lists] = (flipped - head.astype(jnp.float32)).astype(jnp.bfloat16)

    wide = 2 * LANES
    lane = lax.broadcasted_iota(jnp.int32, (1, GROUP), 1)

    def subtract(g):
        chosen = hot[g]
        weight = jnp.where(lane < used - g * GROUP, 1.0, 0.0)
        both = jnp.concatenate([chosen, chosen], axis=0)
        resids = []
        for j in range(width // wide):
            at = slice(j * wide, (j + 1) * wide)
            picked = jnp.dot(parts[at], both, preferred_element_type=jnp.float32)
            resids.append(((turned[g, at].astype(jnp.float32) - picked) * weight).astype(jnp.bfloat16))
        for j in range(width // wide):
            turned[g, j * wide : (j + 1) * wide] = resids[j]

    def multiply(g):
        resids = [turned[g, j * wide : (j + 1) * wide] for j in range(width // wide)]
        return [
            lax.dot_general(r, r, (((1,), (1,)), ((), ())), preferred_element_type=jnp.float32)
            for r in resids
        ]

    subtract(0)

    def encode(g, carry):
        squares = multiply(g)
        subtract(g + 1)
        for j in range(width // wide):
            gram[j] += squares[j]
        return carry

    lax.fori_loop(0, groups - 1, encode, 0)
    squares = multiply(groups - 1)
    for j in range(width // wide):
        gram[j] += squares[j]

    sub = (packed_ref.shape[0] - 8) // (chunks // 2)
    across = LANES // sub
    row = lax.broadcasted_iota(jnp.int32, (sub, LANES), 0)
    lane = lax.broadcasted_iota(jnp.int32, (sub, LANES), 1)
    squares = []
    for q in range(chunks):
        half = slice((q % 2) * LANES, (q % 2 + 1) * LANES)
        square = jnp.zeros((sub, LANES), jnp.float32)
        for a in range(across):
            top = ((q % 2) * across + a) * sub
            square = jnp.where(lane // sub == a, gram[q // 2, top : top + sub, half], square)
        squares.append(square)
    half = chunks // 2
    diagonals = []
    for q in range(half):
        packed_ref[q * sub : (q + 1) * sub, :] = jnp.where(
            row <= lane % sub, squares[q], squares[half + q]
        )
        diagonals.append(
            jnp.sum(jnp.where(row == lane % sub, squares[half + q], 0.0), axis=0, keepdims=True)
        )
    diagonals.append(jnp.zeros((8 - half, LANES), jnp.float32))
    packed_ref[half * sub :, :] = jnp.concatenate(diagonals, axis=0)

    write.wait()


def update_lists(recv, old, blk, sub):
    slots, height, _ = recv.shape
    lists, width = old.shape
    rows = slots * blk
    groups = rows // GROUP
    chunks = width // LANES
    return pl.pallas_call(
        functools.partial(update_kernel, blk),
        out_shape=(
            jax.ShapeDtypeStruct((lists, width), jnp.float32),
            jax.ShapeDtypeStruct((groups + 1, width, GROUP), jnp.bfloat16),
            jax.ShapeDtypeStruct((8, slots), jnp.int32),
            jax.ShapeDtypeStruct((chunks // 2 * sub + 8, LANES), jnp.float32),
            jax.ShapeDtypeStruct((8, LANES), jnp.float32),
        ),
        in_specs=[
            pl.BlockSpec(memory_space=pl.ANY),
            pl.BlockSpec(memory_space=pl.ANY),
        ],
        out_specs=(
            pl.BlockSpec(memory_space=pl.ANY),
            pl.BlockSpec(memory_space=pltpu.VMEM),
            pl.BlockSpec(memory_space=pltpu.VMEM),
            pl.BlockSpec(memory_space=pltpu.VMEM),
            pl.BlockSpec(memory_space=pltpu.VMEM),
        ),
        scratch_shapes=[
            pltpu.VMEM((8, slots // 8, chunks * blk, LANES), jnp.bfloat16),
            pltpu.VMEM((slots, META, LANES), jnp.bfloat16),
            pltpu.VMEM((lists, width), jnp.float32),
            pltpu.VMEM((chunks + 1, rows + GROUP + blk, LANES), jnp.float32),
            pltpu.VMEM((groups + 1, lists, GROUP), jnp.bfloat16),
            pltpu.VMEM((2, GROUP, width), jnp.bfloat16),
            pltpu.VMEM((LANES, LANES), jnp.float32),
            pltpu.SMEM((8, slots), jnp.int32),
            pltpu.VMEM((lists, width), jnp.float32),
            pltpu.VMEM((lists, LANES), jnp.float32),
            pltpu.VMEM((width, 2 * lists), jnp.bfloat16),
            pltpu.VMEM((width // (2 * LANES), 2 * LANES, 2 * LANES), jnp.float32),
            pltpu.SemaphoreType.DMA((10,)),
        ],
        compiler_params=pltpu.CompilerParams(vmem_limit_bytes=VMEM),
        name="update_lists",
    )(recv, old)


def error_kernel(sub, part, blk, place_ref, resid_ref, book_ref, *rest):
    before_ref, error_ref = rest[:2] if part else (None, rest[0])
    slot_ref, lines = rest[2:4] if part == len(BOUNDS) - 2 else (None, None)
    subspaces = book_ref.shape[0]
    slots = place_ref.shape[1]
    width = subspaces * sub
    used = place_ref[0, slots - 1] + place_ref[1, slots - 1]
    groups = (used + GROUP - 1) // GROUP
    first, last = (
        (groups * top + rest) // BOUNDS[-1][0] for top, rest in (BOUNDS[part], BOUNDS[part + 1])
    )
    error_ref[...] = before_ref[...] if part else jnp.zeros_like(error_ref)

    ones = jnp.ones((AUG, GROUP), jnp.bfloat16)

    def visit(g, carry):
        norm = jnp.zeros((8, GROUP), jnp.float32)
        least = jnp.zeros((1, GROUP), jnp.float32)
        for m in range(subspaces):
            piece = resid_ref[g, m * sub : (m + 1) * sub, :]
            long = piece.astype(jnp.float32)
            square = long * long
            for k in range(sub // 8):
                norm = norm + square[k * 8 : (k + 1) * 8]
            distance = jnp.dot(
                book_ref[m],
                jnp.concatenate([piece, ones], axis=0),
                preferred_element_type=jnp.float32,
            )
            least = least + jnp.min(distance, axis=0, keepdims=True)
        error = (least + jnp.sum(norm, axis=0, keepdims=True)) / width
        for k in range(GROUP // LANES):
            error_ref[pl.ds(g * (GROUP // LANES) + k, 1), :] = error[:, k * LANES : (k + 1) * LANES]
        return carry

    lax.fori_loop(first, last, visit, 0)

    if slot_ref is not None:
        lane = lax.broadcasted_iota(jnp.int32, (1, LANES), 1)
        for s in range(slots):
            start = place_ref[0, s]
            line = lax.shift_right_logical(start, LANES.bit_length() - 1)
            shift = start & (LANES - 1)
            window = jnp.where(
                lane >= shift, error_ref[pl.ds(line, 1), :], error_ref[pl.ds(line + 1, 1), :]
            )
            window = pltpu.roll(window, (LANES - shift) & (LANES - 1), 1)
            window = jnp.where(lane < place_ref[1, s], window, 0.0)
            lines[s : s + 1, :] = window
        slot_ref[...] = lines[...].T[0:blk]


def row_errors(place, resid, book, before, sub, blk, part):
    groups, width, _ = resid.shape
    subspaces, codes, depth = book.shape
    slots = place.shape[1]
    vmem = pl.BlockSpec(memory_space=pltpu.VMEM)
    out = [jax.ShapeDtypeStruct((slots * blk // LANES + 8, LANES), jnp.float32)]
    scratch = []
    if part == len(BOUNDS) - 2:
        out.append(jax.ShapeDtypeStruct((blk, slots), jnp.float32))
        scratch.append(pltpu.VMEM((slots, LANES), jnp.float32))
    operands = [place, resid, book] + ([before] if part else [])
    return pl.pallas_call(
        functools.partial(error_kernel, sub, part, blk),
        out_shape=tuple(out),
        in_specs=[
            pl.BlockSpec(memory_space=pltpu.SMEM),
            vmem,
            vmem,
            vmem,
        ][: len(operands)],
        out_specs=tuple(vmem for _ in out),
        scratch_shapes=scratch,
        compiler_params=pltpu.CompilerParams(vmem_limit_bytes=SMALL_VMEM),
        cost_estimate=pl.CostEstimate(
            flops=2 * 256 * codes * subspaces * GROUP * 3,
            bytes_accessed=width * GROUP * 2 * 3,
            transcendentals=0,
        ),
        name="row_errors",
    )(*operands)


def unpack_kernel(even_ref, own_ref, one_ref, two_ref, three_ref, total_ref, out_ref):
    sub = out_ref.shape[1]
    across = LANES // sub
    half = out_ref.shape[0] // across // 2
    even = even_ref[0] != 0
    one, three = one_ref[...], three_ref[...]
    packed = (own_ref[...] + jnp.where(even, three, one)) + (two_ref[...] + jnp.where(even, one, three))
    share = 1.0 / total_ref[0:1, 0:1]
    row = lax.broadcasted_iota(jnp.int32, (sub, sub), 0)
    lane = lax.broadcasted_iota(jnp.int32, (sub, sub), 1)
    for q in range(half):
        square = packed[q * sub : (q + 1) * sub]
        turned = square.T
        for a in range(across):
            at = slice(a * sub, (a + 1) * sub)
            here, flip = square[:, at], turned[at]
            diagonal = packed[half * sub + q : half * sub + q + 1, at]
            out_ref[q * across + a] = jnp.where(row <= lane, here, flip) * share
            other = jnp.where(row > lane, here, jnp.where(row < lane, flip, diagonal))
            out_ref[(half + q) * across + a] = other * share


def unpack_moments(terms, even, total, subspaces, sub):
    return pl.pallas_call(
        unpack_kernel,
        out_shape=jax.ShapeDtypeStruct((subspaces, sub, sub), jnp.float32),
        in_specs=[pl.BlockSpec(memory_space=pltpu.SMEM)] + [pl.BlockSpec(memory_space=pltpu.VMEM)] * 5,
        compiler_params=pltpu.CompilerParams(vmem_limit_bytes=SMALL_VMEM),
        name="unpack_moments",
    )(even, *terms, total)


def extended_book(codebook):
    values = codebook.astype(jnp.float32)
    rest = jnp.sum(jnp.square(values), axis=1)
    parts = []
    for _ in range(3):
        part = lax.reduce_precision(rest, 8, 7)
        parts.append(part)
        rest = rest - part
    parts = jnp.stack(parts, axis=2)
    parts = jnp.pad(parts, ((0, 0), (0, 0), (0, AUG - 3)))
    return jnp.concatenate([-2.0 * values.transpose(0, 2, 1), parts], axis=2).astype(jnp.bfloat16)


def body(vectors, row_list, block_owner, block_fill, old_centroids, codebook):
    devices = lax.axis_size("dev")
    blk = row_list.shape[0] // block_owner.shape[0]
    sub = codebook.shape[1]
    width = vectors.shape[1]
    book = extended_book(codebook)
    send = build_send(vectors, row_list, block_owner, block_fill, devices)
    recv = lax.all_to_all(send, "dev", split_axis=0, concat_axis=0, tiled=True)
    centroids, resid, place, packed, total = update_lists(recv, old_centroids, blk, sub)
    errors, slot_error = None, None
    for part in range(len(BOUNDS) - 1):
        out = row_errors(place, resid, book, errors, sub, blk, part)
        errors, slot_error = out[0], out[-1]

    me = lax.axis_index("dev")

    def shifted(values, stride, step, size):
        pairs = []
        for i in range(devices):
            digit = i // stride % size
            pairs.append((i, i + ((digit + step) % size - digit) * stride))
        return lax.ppermute(values, "dev", pairs)

    packed = packed + shifted(packed, 1, 1, 2)
    stride = 2
    while True:
        two, one, three = (shifted(packed, stride, k, 4) for k in (2, 1, 3))
        even = me // stride % 2 == 0
        terms = (packed, jnp.where(even, three, one), two, jnp.where(even, one, three))
        stride *= 4
        if stride >= devices:
            break
        packed = (terms[0] + terms[1]) + (terms[2] + terms[3])
    moments = unpack_moments((packed, one, two, three), even.astype(jnp.int32).reshape(1), total, codebook.shape[0], sub)
    return centroids, slot_error.T, moments


def solution(mesh):
    return jax.shard_map(
        body,
        mesh=mesh,
        in_specs=(P("dev", None), P("dev"), P("dev"), P("dev"), P("dev", None), P()),
        out_specs=(P("dev", None), P("dev", None), P()),
        check_vma=False,
    )
```

```python
import functools

import jax
import jax.numpy as jnp
from jax import lax
from jax.experimental import pallas as pl
from jax.experimental.pallas import tpu as pltpu
from jax.sharding import PartitionSpec as P

LANES = 128
META = 8
AUG = 16
GROUP = 256
VMEM = 37 * 1024 * 1024
LARGE_VMEM = 56 * 1024 * 1024
SMALL_VMEM = 10 * 1024 * 1024
BOUNDS = ((0, 0), (1, 8), (4, 8), (7, 4), (9, 0))


def send_kernel(
    blk, owner_hbm, fill_hbm, vec_ref, list_hbm, send_ref, owner_ref, fill_ref, list_ref, held, tiles, meta, sems
):
    blocks = owner_ref.shape[0]
    width = vec_ref.shape[1]
    small = [
        pltpu.make_async_copy(source, target, sems.at[blocks + 5 + i])
        for i, (source, target) in enumerate(
            ((owner_hbm, owner_ref), (fill_hbm, fill_ref), (list_hbm, list_ref))
        )
    ]
    for copy in small:
        copy.start()
    chunks = width // LANES
    span = LANES // blk
    me = lax.axis_index("dev")
    place = lax.rem(me, span)
    stages = held.shape[0]
    some = blocks // stages
    loads = [
        pltpu.make_async_copy(
            vec_ref.at[pl.ds(c * some * blk, some * blk), :], held.at[c], sems.at[blocks + 1 + c]
        )
        for c in range(stages)
    ]
    for load in loads:
        load.start()
    for copy in small:
        copy.wait()
    total = functools.reduce(lambda a, b: a + b, [fill_ref[b] for b in range(blocks)])
    rows = lax.broadcasted_iota(jnp.int32, (META, LANES), 0)
    lane = lax.broadcasted_iota(jnp.int32, (1, LANES), 1)
    base = jnp.where(rows == 3, total >> 8, jnp.where(rows == 4, total & 255, 0))
    meta[...] = jnp.broadcast_to(base.astype(jnp.float32).astype(jnp.bfloat16)[None], meta.shape)
    for b in range(blocks):
        line = list_ref[b // span : b // span + 1, :] + 1
        line = pltpu.roll(line, lax.rem(place + span - b % span, span) * blk, 1)
        kept = (lane // blk == place) & (lax.rem(lane, blk) < fill_ref[b])
        line = jnp.broadcast_to(jnp.where(kept, line, 0), (META, LANES))
        count = jnp.broadcast_to(jnp.where(lane == me, fill_ref[b], 0), (META, LANES))
        tile = jnp.where(
            rows == 0, line & 255, jnp.where(rows == 1, line >> 8, jnp.where(rows == 2, count, base))
        )
        meta[owner_ref[b]] = tile.astype(jnp.float32).astype(jnp.bfloat16)
    last = pltpu.make_async_copy(
        meta, send_ref.at[:, pl.ds(chunks * blk, META), :], sems.at[blocks]
    )
    last.start()
    copies = []
    for c in range(stages):
        loads[c].wait()
        for b in range(c * some, (c + 1) * some):
            at = slice((b - c * some) * blk, (b - c * some + 1) * blk)
            for j in range(chunks):
                tiles[b, j * blk : (j + 1) * blk, :] = held[c, at, j * LANES : (j + 1) * LANES]
            copy = pltpu.make_async_copy(
                tiles.at[b], send_ref.at[owner_ref[b], pl.ds(0, chunks * blk), :], sems.at[b]
            )
            copy.start()
            copies.append(copy)
    for copy in copies:
        copy.wait()
    last.wait()


def build_send(vectors, row_list, block_owner, block_fill, devices):
    rows, width = vectors.shape
    blocks = block_owner.shape[0]
    blk = rows // blocks
    height = width // LANES * blk
    return pl.pallas_call(
        functools.partial(send_kernel, blk),
        out_shape=jax.ShapeDtypeStruct((devices, height + META, LANES), jnp.bfloat16),
        in_specs=[pl.BlockSpec(memory_space=pl.ANY)] * 4,
        out_specs=pl.BlockSpec(memory_space=pl.ANY),
        scratch_shapes=[
            pltpu.SMEM((blocks,), jnp.int32),
            pltpu.SMEM((blocks,), jnp.int32),
            pltpu.VMEM((rows // LANES, LANES), jnp.int32),
            pltpu.VMEM((4, rows // 4, width), jnp.bfloat16),
            pltpu.VMEM((blocks, height, LANES), jnp.bfloat16),
            pltpu.VMEM((devices, META, LANES), jnp.bfloat16),
            pltpu.SemaphoreType.DMA((blocks + 8,)),
        ],
        compiler_params=pltpu.CompilerParams(vmem_limit_bytes=LARGE_VMEM),
        name="build_send",
    )(block_owner, block_fill, vectors, row_list.reshape(rows // LANES, LANES))


def update_kernel(
    blk, recv_ref, old_ref, cent_ref, turned, where_ref, packed_ref, total_ref,
    blocks, info, dense, hot, values, column, place_ref, sums, counts, parts, gram, sems,
):
    slots, height, _ = recv_ref.shape
    lists, width = old_ref.shape
    chunks = width // LANES
    span = LANES // blk
    some = slots // blocks.shape[0]
    rows = slots * blk

    notes = pltpu.make_async_copy(recv_ref.at[:, pl.ds(chunks * blk, META), :], info, sems.at[0])
    notes.start()

    def fetch(c):
        return pltpu.make_async_copy(
            recv_ref.at[pl.ds(c * some, some), pl.ds(0, chunks * blk), :], blocks.at[c], sems.at[1 + c]
        )

    for c in range(blocks.shape[0]):
        fetch(c).start()

    notes.wait()
    lines, seen = [], jnp.zeros((META, LANES), jnp.float32)
    for q in range(slots // span):
        note = info[q * span].astype(jnp.float32)
        for s in range(1, span):
            note = note + info[q * span + s].astype(jnp.float32)
        lines.append(note[0:1] + 256.0 * note[1:2])
        seen = seen + note
    fill = jnp.broadcast_to(seen[2:3], (8, LANES))
    before = lax.broadcasted_iota(jnp.int32, (slots, slots), 0)
    after = lax.broadcasted_iota(jnp.int32, (slots, slots), 1)
    start = jnp.dot(
        fill.astype(jnp.bfloat16),
        jnp.where(before < after, 1.0, 0.0).astype(jnp.bfloat16),
        preferred_element_type=jnp.float32,
    )
    which = lax.broadcasted_iota(jnp.int32, (8, slots), 0)
    where_ref[...] = jnp.where(which == 0, start, fill).astype(jnp.int32)
    mover = pltpu.make_async_copy(where_ref, place_ref, sems.at[0])
    mover.start()
    total_ref[...] = jnp.broadcast_to(seen[4:5] + 256.0 * seen[3:4], total_ref.shape)
    lines.append(jnp.zeros((LANES - len(lines), LANES), jnp.float32))
    column[...] = jnp.concatenate(lines, axis=0).T
    sums[...] = jnp.zeros_like(sums)
    counts[...] = jnp.zeros_like(counts)
    gram[...] = jnp.zeros_like(gram)
    mover.wait()

    lane = lax.broadcasted_iota(jnp.int32, (blk, LANES), 1)

    def pack(c, carry):
        fetch(c).wait()
        for s in range(some):
            at = pl.ds(place_ref[0, c * some + s], blk)
            for j in range(chunks):
                dense[j, at, :] = blocks[c, s, j * blk : (j + 1) * blk, :].astype(jnp.float32)
            ids = column[(s % span) * blk : (s % span + 1) * blk, :]
            dense[chunks, at, :] = jnp.where(lane == c * (some // span) + s // span, ids, 0.0)
        return carry

    lax.fori_loop(0, blocks.shape[0], pack, 0)
    used = place_ref[0, slots - 1] + place_ref[1, slots - 1]
    for j in range(chunks + 1):
        dense[j, pl.ds(used, GROUP + blk), :] = jnp.zeros((GROUP + blk, LANES), jnp.float32)
    groups = jnp.maximum((used + GROUP - 1) // GROUP, 1)

    def prepare(g):
        at = pl.ds(pl.multiple_of(g * GROUP, GROUP), GROUP)
        code = jnp.sum(dense[chunks, at, :].T[0 : slots // span], axis=0, keepdims=True)
        ids = lax.broadcasted_iota(jnp.int32, (lists, GROUP), 0).astype(jnp.float32) + 1.0
        hot[g] = jnp.where(ids == code, 1.0, 0.0).astype(jnp.bfloat16)
        for j in range(chunks):
            piece = dense[j, at, :].astype(jnp.bfloat16)
            turned[g, j * LANES : (j + 1) * LANES, :] = piece.T
            values[g & 1, :, j * LANES : (j + 1) * LANES] = piece

    prepare(0)

    def gather(g, carry):
        chosen = hot[g]
        added = jnp.dot(chosen, values[g & 1], preferred_element_type=jnp.float32)
        part = chosen[:, 0:LANES].astype(jnp.float32)
        for k in range(1, GROUP // LANES):
            part = part + chosen[:, k * LANES : (k + 1) * LANES].astype(jnp.float32)
        prepare(g + 1)
        sums[...] += added
        counts[...] += part
        return carry

    lax.fori_loop(0, groups, gather, 0)

    share = 1.0 / (jnp.sum(counts[...], axis=1, keepdims=True) + 1.0)
    cent = (sums[...] + old_ref[...]) * share
    sums[...] = cent
    write = pltpu.make_async_copy(sums, cent_ref, sems.at[0])
    write.start()
    flipped = cent.T
    head = flipped.astype(jnp.bfloat16)
    parts[:, 0:lists] = head
    parts[:, lists : 2 * lists] = (flipped - head.astype(jnp.float32)).astype(jnp.bfloat16)

    wide = 2 * LANES
    lane = lax.broadcasted_iota(jnp.int32, (1, GROUP), 1)

    def subtract(g):
        chosen = hot[g]
        weight = jnp.where(lane < used - g * GROUP, 1.0, 0.0)
        both = jnp.concatenate([chosen, chosen], axis=0)
        resids = []
        for j in range(width // wide):
            at = slice(j * wide, (j + 1) * wide)
            picked = jnp.dot(parts[at], both, preferred_element_type=jnp.float32)
            resids.append(((turned[g, at].astype(jnp.float32) - picked) * weight).astype(jnp.bfloat16))
        for j in range(width // wide):
            turned[g, j * wide : (j + 1) * wide] = resids[j]

    def multiply(g):
        resids = [turned[g, j * wide : (j + 1) * wide] for j in range(width // wide)]
        return [
            lax.dot_general(r, r, (((1,), (1,)), ((), ())), preferred_element_type=jnp.float32)
            for r in resids
        ]

    subtract(0)

    def encode(g, carry):
        squares = multiply(g)
        subtract(g + 1)
        for j in range(width // wide):
            gram[j] += squares[j]
        return carry

    lax.fori_loop(0, groups - 1, encode, 0)
    squares = multiply(groups - 1)
    for j in range(width // wide):
        gram[j] += squares[j]

    sub = (packed_ref.shape[0] - 8) // (chunks // 2)
    across = LANES // sub
    row = lax.broadcasted_iota(jnp.int32, (sub, LANES), 0)
    lane = lax.broadcasted_iota(jnp.int32, (sub, LANES), 1)
    squares = []
    for q in range(chunks):
        half = slice((q % 2) * LANES, (q % 2 + 1) * LANES)
        square = jnp.zeros((sub, LANES), jnp.float32)
        for a in range(across):
            top = ((q % 2) * across + a) * sub
            square = jnp.where(lane // sub == a, gram[q // 2, top : top + sub, half], square)
        squares.append(square)
    half = chunks // 2
    diagonals = []
    for q in range(half):
        packed_ref[q * sub : (q + 1) * sub, :] = jnp.where(
            row <= lane % sub, squares[q], squares[half + q]
        )
        diagonals.append(
            jnp.sum(jnp.where(row == lane % sub, squares[half + q], 0.0), axis=0, keepdims=True)
        )
    diagonals.append(jnp.zeros((8 - half, LANES), jnp.float32))
    packed_ref[half * sub :, :] = jnp.concatenate(diagonals, axis=0)

    write.wait()


def update_lists(recv, old, blk, sub):
    slots, height, _ = recv.shape
    lists, width = old.shape
    rows = slots * blk
    groups = rows // GROUP
    chunks = width // LANES
    return pl.pallas_call(
        functools.partial(update_kernel, blk),
        out_shape=(
            jax.ShapeDtypeStruct((lists, width), jnp.float32),
            jax.ShapeDtypeStruct((groups + 1, width, GROUP), jnp.bfloat16),
            jax.ShapeDtypeStruct((8, slots), jnp.int32),
            jax.ShapeDtypeStruct((chunks // 2 * sub + 8, LANES), jnp.float32),
            jax.ShapeDtypeStruct((8, LANES), jnp.float32),
        ),
        in_specs=[
            pl.BlockSpec(memory_space=pl.ANY),
            pl.BlockSpec(memory_space=pltpu.VMEM),
        ],
        out_specs=(
            pl.BlockSpec(memory_space=pl.ANY),
            pl.BlockSpec(memory_space=pltpu.VMEM),
            pl.BlockSpec(memory_space=pltpu.VMEM),
            pl.BlockSpec(memory_space=pltpu.VMEM),
            pl.BlockSpec(memory_space=pltpu.VMEM),
        ),
        scratch_shapes=[
            pltpu.VMEM((8, slots // 8, chunks * blk, LANES), jnp.bfloat16),
            pltpu.VMEM((slots, META, LANES), jnp.bfloat16),
            pltpu.VMEM((chunks + 1, rows + GROUP + blk, LANES), jnp.float32),
            pltpu.VMEM((groups + 1, lists, GROUP), jnp.bfloat16),
            pltpu.VMEM((2, GROUP, width), jnp.bfloat16),
            pltpu.VMEM((LANES, LANES), jnp.float32),
            pltpu.SMEM((8, slots), jnp.int32),
            pltpu.VMEM((lists, width), jnp.float32),
            pltpu.VMEM((lists, LANES), jnp.float32),
            pltpu.VMEM((width, 2 * lists), jnp.bfloat16),
            pltpu.VMEM((width // (2 * LANES), 2 * LANES, 2 * LANES), jnp.float32),
            pltpu.SemaphoreType.DMA((10,)),
        ],
        compiler_params=pltpu.CompilerParams(vmem_limit_bytes=VMEM),
        name="update_lists",
    )(recv, old)


def error_kernel(sub, part, blk, place_ref, resid_ref, book_ref, *rest):
    before_ref, error_ref = rest[:2] if part else (None, rest[0])
    slot_ref, lines = rest[2:4] if part == len(BOUNDS) - 2 else (None, None)
    subspaces = book_ref.shape[0]
    slots = place_ref.shape[1]
    width = subspaces * sub
    used = place_ref[0, slots - 1] + place_ref[1, slots - 1]
    groups = (used + GROUP - 1) // GROUP
    first, last = (
        (groups * top + rest) // BOUNDS[-1][0] for top, rest in (BOUNDS[part], BOUNDS[part + 1])
    )
    error_ref[...] = before_ref[...] if part else jnp.zeros_like(error_ref)

    ones = jnp.ones((AUG, GROUP), jnp.bfloat16)

    def visit(g, carry):
        norm = jnp.zeros((8, GROUP), jnp.float32)
        least = jnp.zeros((1, GROUP), jnp.float32)
        for m in range(subspaces):
            piece = resid_ref[g, m * sub : (m + 1) * sub, :]
            long = piece.astype(jnp.float32)
            square = long * long
            for k in range(sub // 8):
                norm = norm + square[k * 8 : (k + 1) * 8]
            distance = jnp.dot(
                book_ref[m],
                jnp.concatenate([piece, ones], axis=0),
                preferred_element_type=jnp.float32,
            )
            least = least + jnp.min(distance, axis=0, keepdims=True)
        error = (least + jnp.sum(norm, axis=0, keepdims=True)) / width
        for k in range(GROUP // LANES):
            error_ref[pl.ds(g * (GROUP // LANES) + k, 1), :] = error[:, k * LANES : (k + 1) * LANES]
        return carry

    lax.fori_loop(first, last, visit, 0)

    if slot_ref is not None:
        lane = lax.broadcasted_iota(jnp.int32, (1, LANES), 1)
        for s in range(slots):
            start = place_ref[0, s]
            line = lax.shift_right_logical(start, LANES.bit_length() - 1)
            shift = start & (LANES - 1)
            window = jnp.where(
                lane >= shift, error_ref[pl.ds(line, 1), :], error_ref[pl.ds(line + 1, 1), :]
            )
            window = pltpu.roll(window, (LANES - shift) & (LANES - 1), 1)
            window = jnp.where(lane < place_ref[1, s], window, 0.0)
            lines[s : s + 1, :] = window
        slot_ref[...] = lines[...].T[0:blk]


def row_errors(place, resid, book, before, sub, blk, part):
    groups, width, _ = resid.shape
    subspaces, codes, depth = book.shape
    slots = place.shape[1]
    vmem = pl.BlockSpec(memory_space=pltpu.VMEM)
    out = [jax.ShapeDtypeStruct((slots * blk // LANES + 8, LANES), jnp.float32)]
    scratch = []
    if part == len(BOUNDS) - 2:
        out.append(jax.ShapeDtypeStruct((blk, slots), jnp.float32))
        scratch.append(pltpu.VMEM((slots, LANES), jnp.float32))
    operands = [place, resid, book] + ([before] if part else [])
    return pl.pallas_call(
        functools.partial(error_kernel, sub, part, blk),
        out_shape=tuple(out),
        in_specs=[
            pl.BlockSpec(memory_space=pltpu.SMEM),
            vmem,
            vmem,
            vmem,
        ][: len(operands)],
        out_specs=tuple(vmem for _ in out),
        scratch_shapes=scratch,
        compiler_params=pltpu.CompilerParams(vmem_limit_bytes=SMALL_VMEM),
        cost_estimate=pl.CostEstimate(
            flops=2 * 256 * codes * subspaces * GROUP * 3,
            bytes_accessed=width * GROUP * 2 * 3,
            transcendentals=0,
        ),
        name="row_errors",
    )(*operands)


def unpack_kernel(even_ref, own_ref, one_ref, two_ref, three_ref, total_ref, out_ref):
    sub = out_ref.shape[1]
    across = LANES // sub
    half = out_ref.shape[0] // across // 2
    even = even_ref[0] != 0
    one, three = one_ref[...], three_ref[...]
    packed = (own_ref[...] + jnp.where(even, three, one)) + (two_ref[...] + jnp.where(even, one, three))
    share = 1.0 / total_ref[0:1, 0:1]
    row = lax.broadcasted_iota(jnp.int32, (sub, sub), 0)
    lane = lax.broadcasted_iota(jnp.int32, (sub, sub), 1)
    for q in range(half):
        square = packed[q * sub : (q + 1) * sub]
        turned = square.T
        for a in range(across):
            at = slice(a * sub, (a + 1) * sub)
            here, flip = square[:, at], turned[at]
            diagonal = packed[half * sub + q : half * sub + q + 1, at]
            out_ref[q * across + a] = jnp.where(row <= lane, here, flip) * share
            other = jnp.where(row > lane, here, jnp.where(row < lane, flip, diagonal))
            out_ref[(half + q) * across + a] = other * share


def unpack_moments(terms, even, total, subspaces, sub):
    return pl.pallas_call(
        unpack_kernel,
        out_shape=jax.ShapeDtypeStruct((subspaces, sub, sub), jnp.float32),
        in_specs=[pl.BlockSpec(memory_space=pltpu.SMEM)] + [pl.BlockSpec(memory_space=pltpu.VMEM)] * 5,
        compiler_params=pltpu.CompilerParams(vmem_limit_bytes=SMALL_VMEM),
        name="unpack_moments",
    )(even, *terms, total)


def extended_book(codebook):
    values = codebook.astype(jnp.float32)
    rest = jnp.sum(jnp.square(values), axis=1)
    parts = []
    for _ in range(3):
        part = lax.reduce_precision(rest, 8, 7)
        parts.append(part)
        rest = rest - part
    parts = jnp.stack(parts, axis=2)
    parts = jnp.pad(parts, ((0, 0), (0, 0), (0, AUG - 3)))
    return jnp.concatenate([-2.0 * values.transpose(0, 2, 1), parts], axis=2).astype(jnp.bfloat16)


def body(vectors, row_list, block_owner, block_fill, old_centroids, codebook):
    devices = lax.axis_size("dev")
    blk = row_list.shape[0] // block_owner.shape[0]
    sub = codebook.shape[1]
    width = vectors.shape[1]
    book = extended_book(codebook)
    send = build_send(vectors, row_list, block_owner, block_fill, devices)
    recv = lax.all_to_all(send, "dev", split_axis=0, concat_axis=0, tiled=True)
    centroids, resid, place, packed, total = update_lists(recv, old_centroids, blk, sub)
    errors, slot_error = None, None
    for part in range(len(BOUNDS) - 1):
        out = row_errors(place, resid, book, errors, sub, blk, part)
        errors, slot_error = out[0], out[-1]

    me = lax.axis_index("dev")

    def shifted(values, stride, step, size):
        pairs = []
        for i in range(devices):
            digit = i // stride % size
            pairs.append((i, i + ((digit + step) % size - digit) * stride))
        return lax.ppermute(values, "dev", pairs)

    packed = packed + shifted(packed, 1, 1, 2)
    stride = 2
    while True:
        three, one, two = (shifted(packed, stride, k, 4) for k in (3, 1, 2))
        even = me // stride % 2 == 0
        terms = (packed, jnp.where(even, three, one), two, jnp.where(even, one, three))
        stride *= 4
        if stride >= devices:
            break
        packed = (terms[0] + terms[1]) + (terms[2] + terms[3])
    moments = unpack_moments((packed, one, two, three), even.astype(jnp.int32).reshape(1), total, codebook.shape[0], sub)
    return centroids, slot_error.T, moments


def solution(mesh):
    return jax.shard_map(
        body,
        mesh=mesh,
        in_specs=(P("dev", None), P("dev"), P("dev"), P("dev"), P("dev", None), P()),
        out_specs=(P("dev", None), P("dev", None), P()),
        check_vma=False,
    )
```

```python
import functools

import jax
import jax.numpy as jnp
from jax import lax
from jax.experimental import pallas as pl
from jax.experimental.pallas import tpu as pltpu
from jax.sharding import PartitionSpec as P

LANES = 128
META = 8
AUG = 16
GROUP = 256
VMEM = 37 * 1024 * 1024
LARGE_VMEM = 56 * 1024 * 1024
SMALL_VMEM = 10 * 1024 * 1024
BOUNDS = ((0, 0), (1, 8), (4, 8), (7, 4), (9, 0))


def send_kernel(
    blk, owner_hbm, fill_hbm, vec_ref, list_hbm, send_ref, owner_ref, fill_ref, list_ref, held, tiles, meta, sems
):
    blocks = owner_ref.shape[0]
    width = vec_ref.shape[1]
    small = [
        pltpu.make_async_copy(source, target, sems.at[blocks + 5 + i])
        for i, (source, target) in enumerate(
            ((owner_hbm, owner_ref), (fill_hbm, fill_ref), (list_hbm, list_ref))
        )
    ]
    for copy in small:
        copy.start()
    chunks = width // LANES
    span = LANES // blk
    me = lax.axis_index("dev")
    place = lax.rem(me, span)
    stages = held.shape[0]
    some = blocks // stages
    loads = [
        pltpu.make_async_copy(
            vec_ref.at[pl.ds(c * some * blk, some * blk), :], held.at[c], sems.at[blocks + 1 + c]
        )
        for c in range(stages)
    ]
    for load in loads:
        load.start()
    for copy in small:
        copy.wait()
    total = functools.reduce(lambda a, b: a + b, [fill_ref[b] for b in range(blocks)])
    rows = lax.broadcasted_iota(jnp.int32, (META, LANES), 0)
    lane = lax.broadcasted_iota(jnp.int32, (1, LANES), 1)
    base = jnp.where(rows == 3, total >> 8, jnp.where(rows == 4, total & 255, 0))
    meta[...] = jnp.broadcast_to(base.astype(jnp.float32).astype(jnp.bfloat16)[None], meta.shape)
    for b in range(blocks):
        line = list_ref[b // span : b // span + 1, :] + 1
        line = pltpu.roll(line, lax.rem(place + span - b % span, span) * blk, 1)
        kept = (lane // blk == place) & (lax.rem(lane, blk) < fill_ref[b])
        line = jnp.broadcast_to(jnp.where(kept, line, 0), (META, LANES))
        count = jnp.broadcast_to(jnp.where(lane == me, fill_ref[b], 0), (META, LANES))
        tile = jnp.where(
            rows == 0, line & 255, jnp.where(rows == 1, line >> 8, jnp.where(rows == 2, count, base))
        )
        meta[owner_ref[b]] = tile.astype(jnp.float32).astype(jnp.bfloat16)
    last = pltpu.make_async_copy(
        meta, send_ref.at[:, pl.ds(chunks * blk, META), :], sems.at[blocks]
    )
    last.start()
    copies = []
    for c in range(stages):
        loads[c].wait()
        for b in range(c * some, (c + 1) * some):
            at = slice((b - c * some) * blk, (b - c * some + 1) * blk)
            for j in range(chunks):
                tiles[b, j * blk : (j + 1) * blk, :] = held[c, at, j * LANES : (j + 1) * LANES]
            copy = pltpu.make_async_copy(
                tiles.at[b], send_ref.at[owner_ref[b], pl.ds(0, chunks * blk), :], sems.at[b]
            )
            copy.start()
            copies.append(copy)
    for copy in copies:
        copy.wait()
    last.wait()


def build_send(vectors, row_list, block_owner, block_fill, devices):
    rows, width = vectors.shape
    blocks = block_owner.shape[0]
    blk = rows // blocks
    height = width // LANES * blk
    return pl.pallas_call(
        functools.partial(send_kernel, blk),
        out_shape=jax.ShapeDtypeStruct((devices, height + META, LANES), jnp.bfloat16),
        in_specs=[pl.BlockSpec(memory_space=pl.ANY)] * 4,
        out_specs=pl.BlockSpec(memory_space=pl.ANY),
        scratch_shapes=[
            pltpu.SMEM((blocks,), jnp.int32),
            pltpu.SMEM((blocks,), jnp.int32),
            pltpu.VMEM((rows // LANES, LANES), jnp.int32),
            pltpu.VMEM((4, rows // 4, width), jnp.bfloat16),
            pltpu.VMEM((blocks, height, LANES), jnp.bfloat16),
            pltpu.VMEM((devices, META, LANES), jnp.bfloat16),
            pltpu.SemaphoreType.DMA((blocks + 8,)),
        ],
        compiler_params=pltpu.CompilerParams(vmem_limit_bytes=LARGE_VMEM),
        name="build_send",
    )(block_owner, block_fill, vectors, row_list.reshape(rows // LANES, LANES))


def update_kernel(
    blk, recv_ref, old_ref, cent_ref, turned, where_ref, packed_ref, total_ref,
    blocks, info, dense, hot, values, column, place_ref, sums, counts, parts, gram, sems,
):
    slots, height, _ = recv_ref.shape
    lists, width = old_ref.shape
    chunks = width // LANES
    span = LANES // blk
    some = slots // blocks.shape[0]
    rows = slots * blk

    notes = pltpu.make_async_copy(recv_ref.at[:, pl.ds(chunks * blk, META), :], info, sems.at[0])
    notes.start()

    def fetch(c):
        return pltpu.make_async_copy(
            recv_ref.at[pl.ds(c * some, some), pl.ds(0, chunks * blk), :], blocks.at[c], sems.at[1 + c]
        )

    for c in range(blocks.shape[0]):
        fetch(c).start()

    notes.wait()
    lines, seen = [], jnp.zeros((META, LANES), jnp.float32)
    for q in range(slots // span):
        note = info[q * span].astype(jnp.float32)
        for s in range(1, span):
            note = note + info[q * span + s].astype(jnp.float32)
        lines.append(note[0:1] + 256.0 * note[1:2])
        seen = seen + note
    fill = jnp.broadcast_to(seen[2:3], (8, LANES))
    before = lax.broadcasted_iota(jnp.int32, (slots, slots), 0)
    after = lax.broadcasted_iota(jnp.int32, (slots, slots), 1)
    start = jnp.dot(
        fill.astype(jnp.bfloat16),
        jnp.where(before < after, 1.0, 0.0).astype(jnp.bfloat16),
        preferred_element_type=jnp.float32,
    )
    which = lax.broadcasted_iota(jnp.int32, (8, slots), 0)
    where_ref[...] = jnp.where(which == 0, start, fill).astype(jnp.int32)
    mover = pltpu.make_async_copy(where_ref, place_ref, sems.at[0])
    mover.start()
    total_ref[...] = jnp.broadcast_to(seen[4:5] + 256.0 * seen[3:4], total_ref.shape)
    lines.append(jnp.zeros((LANES - len(lines), LANES), jnp.float32))
    column[...] = jnp.concatenate(lines, axis=0).T
    sums[...] = jnp.zeros_like(sums)
    counts[...] = jnp.zeros_like(counts)
    gram[...] = jnp.zeros_like(gram)
    mover.wait()

    lane = lax.broadcasted_iota(jnp.int32, (blk, LANES), 1)

    def pack(c, carry):
        fetch(c).wait()
        for s in range(some):
            at = pl.ds(place_ref[0, c * some + s], blk)
            for j in range(chunks):
                dense[j, at, :] = blocks[c, s, j * blk : (j + 1) * blk, :].astype(jnp.float32)
            ids = column[(s % span) * blk : (s % span + 1) * blk, :]
            dense[chunks, at, :] = jnp.where(lane == c * (some // span) + s // span, ids, 0.0)
        return carry

    lax.fori_loop(0, blocks.shape[0], pack, 0)
    used = place_ref[0, slots - 1] + place_ref[1, slots - 1]
    for j in range(chunks + 1):
        dense[j, pl.ds(used, GROUP + blk), :] = jnp.zeros((GROUP + blk, LANES), jnp.float32)
    groups = jnp.maximum((used + GROUP - 1) // GROUP, 1)

    def prepare(g):
        at = pl.ds(pl.multiple_of(g * GROUP, GROUP), GROUP)
        code = jnp.sum(dense[chunks, at, :].T[0 : slots // span], axis=0, keepdims=True)
        ids = lax.broadcasted_iota(jnp.int32, (lists, GROUP), 0).astype(jnp.float32) + 1.0
        hot[g] = jnp.where(ids == code, 1.0, 0.0).astype(jnp.bfloat16)
        for j in range(chunks):
            piece = dense[j, at, :].astype(jnp.bfloat16)
            turned[g, j * LANES : (j + 1) * LANES, :] = piece.T
            values[g & 1, :, j * LANES : (j + 1) * LANES] = piece

    prepare(0)

    def add(g):
        chosen = hot[g]
        added = jnp.dot(chosen, values[g & 1], preferred_element_type=jnp.float32)
        part = chosen[:, 0:LANES].astype(jnp.float32)
        for k in range(1, GROUP // LANES):
            part = part + chosen[:, k * LANES : (k + 1) * LANES].astype(jnp.float32)
        return added, part

    def gather(g, carry):
        added, part = add(g)
        prepare(g + 1)
        sums[...] += added
        counts[...] += part
        return carry

    lax.fori_loop(0, groups - 1, gather, 0)
    added, part = add(groups - 1)
    share = 1.0 / (jnp.sum(counts[...] + part, axis=1, keepdims=True) + 1.0)
    cent = (sums[...] + added + old_ref[...]) * share
    sums[...] = cent
    write = pltpu.make_async_copy(sums, cent_ref, sems.at[0])
    write.start()
    flipped = cent.T
    head = flipped.astype(jnp.bfloat16)
    parts[:, 0:lists] = head
    parts[:, lists : 2 * lists] = (flipped - head.astype(jnp.float32)).astype(jnp.bfloat16)

    wide = 2 * LANES
    lane = lax.broadcasted_iota(jnp.int32, (1, GROUP), 1)

    def subtract(g):
        chosen = hot[g]
        weight = jnp.where(lane < used - g * GROUP, 1.0, 0.0)
        both = jnp.concatenate([chosen, chosen], axis=0)
        resids = []
        for j in range(width // wide):
            at = slice(j * wide, (j + 1) * wide)
            picked = jnp.dot(parts[at], both, preferred_element_type=jnp.float32)
            resids.append(((turned[g, at].astype(jnp.float32) - picked) * weight).astype(jnp.bfloat16))
        for j in range(width // wide):
            turned[g, j * wide : (j + 1) * wide] = resids[j]

    def multiply(g):
        resids = [turned[g, j * wide : (j + 1) * wide] for j in range(width // wide)]
        return [
            lax.dot_general(r, r, (((1,), (1,)), ((), ())), preferred_element_type=jnp.float32)
            for r in resids
        ]

    subtract(0)

    def encode(g, carry):
        squares = multiply(g)
        subtract(g + 1)
        for j in range(width // wide):
            gram[j] += squares[j]
        return carry

    lax.fori_loop(0, groups - 1, encode, 0)
    squares = multiply(groups - 1)
    for j in range(width // wide):
        gram[j] += squares[j]

    sub = (packed_ref.shape[0] - 8) // (chunks // 2)
    across = LANES // sub
    row = lax.broadcasted_iota(jnp.int32, (sub, LANES), 0)
    lane = lax.broadcasted_iota(jnp.int32, (sub, LANES), 1)
    squares = []
    for q in range(chunks):
        half = slice((q % 2) * LANES, (q % 2 + 1) * LANES)
        square = jnp.zeros((sub, LANES), jnp.float32)
        for a in range(across):
            top = ((q % 2) * across + a) * sub
            square = jnp.where(lane // sub == a, gram[q // 2, top : top + sub, half], square)
        squares.append(square)
    half = chunks // 2
    diagonals = []
    for q in range(half):
        packed_ref[q * sub : (q + 1) * sub, :] = jnp.where(
            row <= lane % sub, squares[q], squares[half + q]
        )
        diagonals.append(
            jnp.sum(jnp.where(row == lane % sub, squares[half + q], 0.0), axis=0, keepdims=True)
        )
    diagonals.append(jnp.zeros((8 - half, LANES), jnp.float32))
    packed_ref[half * sub :, :] = jnp.concatenate(diagonals, axis=0)

    write.wait()


def update_lists(recv, old, blk, sub):
    slots, height, _ = recv.shape
    lists, width = old.shape
    rows = slots * blk
    groups = rows // GROUP
    chunks = width // LANES
    return pl.pallas_call(
        functools.partial(update_kernel, blk),
        out_shape=(
            jax.ShapeDtypeStruct((lists, width), jnp.float32),
            jax.ShapeDtypeStruct((groups + 1, width, GROUP), jnp.bfloat16),
            jax.ShapeDtypeStruct((8, slots), jnp.int32),
            jax.ShapeDtypeStruct((chunks // 2 * sub + 8, LANES), jnp.float32),
            jax.ShapeDtypeStruct((8, LANES), jnp.float32),
        ),
        in_specs=[
            pl.BlockSpec(memory_space=pl.ANY),
            pl.BlockSpec(memory_space=pltpu.VMEM),
        ],
        out_specs=(
            pl.BlockSpec(memory_space=pl.ANY),
            pl.BlockSpec(memory_space=pltpu.VMEM),
            pl.BlockSpec(memory_space=pltpu.VMEM),
            pl.BlockSpec(memory_space=pltpu.VMEM),
            pl.BlockSpec(memory_space=pltpu.VMEM),
        ),
        scratch_shapes=[
            pltpu.VMEM((8, slots // 8, chunks * blk, LANES), jnp.bfloat16),
            pltpu.VMEM((slots, META, LANES), jnp.bfloat16),
            pltpu.VMEM((chunks + 1, rows + GROUP + blk, LANES), jnp.float32),
            pltpu.VMEM((groups + 1, lists, GROUP), jnp.bfloat16),
            pltpu.VMEM((2, GROUP, width), jnp.bfloat16),
            pltpu.VMEM((LANES, LANES), jnp.float32),
            pltpu.SMEM((8, slots), jnp.int32),
            pltpu.VMEM((lists, width), jnp.float32),
            pltpu.VMEM((lists, LANES), jnp.float32),
            pltpu.VMEM((width, 2 * lists), jnp.bfloat16),
            pltpu.VMEM((width // (2 * LANES), 2 * LANES, 2 * LANES), jnp.float32),
            pltpu.SemaphoreType.DMA((10,)),
        ],
        compiler_params=pltpu.CompilerParams(vmem_limit_bytes=VMEM),
        name="update_lists",
    )(recv, old)


def error_kernel(sub, part, blk, place_ref, resid_ref, book_ref, *rest):
    before_ref, error_ref = rest[:2] if part else (None, rest[0])
    slot_ref, lines = rest[2:4] if part == len(BOUNDS) - 2 else (None, None)
    subspaces = book_ref.shape[0]
    slots = place_ref.shape[1]
    width = subspaces * sub
    used = place_ref[0, slots - 1] + place_ref[1, slots - 1]
    groups = (used + GROUP - 1) // GROUP
    first, last = (
        (groups * top + rest) // BOUNDS[-1][0] for top, rest in (BOUNDS[part], BOUNDS[part + 1])
    )
    error_ref[...] = before_ref[...] if part else jnp.zeros_like(error_ref)

    ones = jnp.ones((AUG, GROUP), jnp.bfloat16)

    def visit(g, carry):
        norm = jnp.zeros((8, GROUP), jnp.float32)
        least = jnp.zeros((1, GROUP), jnp.float32)
        for m in range(subspaces):
            piece = resid_ref[g, m * sub : (m + 1) * sub, :]
            long = piece.astype(jnp.float32)
            square = long * long
            for k in range(sub // 8):
                norm = norm + square[k * 8 : (k + 1) * 8]
            distance = jnp.dot(
                book_ref[m],
                jnp.concatenate([piece, ones], axis=0),
                preferred_element_type=jnp.float32,
            )
            least = least + jnp.min(distance, axis=0, keepdims=True)
        error = (least + jnp.sum(norm, axis=0, keepdims=True)) / width
        for k in range(GROUP // LANES):
            error_ref[pl.ds(g * (GROUP // LANES) + k, 1), :] = error[:, k * LANES : (k + 1) * LANES]
        return carry

    lax.fori_loop(first, last, visit, 0)

    if slot_ref is not None:
        lane = lax.broadcasted_iota(jnp.int32, (1, LANES), 1)
        for s in range(slots):
            start = place_ref[0, s]
            line = lax.shift_right_logical(start, LANES.bit_length() - 1)
            shift = start & (LANES - 1)
            window = jnp.where(
                lane >= shift, error_ref[pl.ds(line, 1), :], error_ref[pl.ds(line + 1, 1), :]
            )
            window = pltpu.roll(window, (LANES - shift) & (LANES - 1), 1)
            window = jnp.where(lane < place_ref[1, s], window, 0.0)
            lines[s : s + 1, :] = window
        slot_ref[...] = lines[...].T[0:blk]


def row_errors(place, resid, book, before, sub, blk, part):
    groups, width, _ = resid.shape
    subspaces, codes, depth = book.shape
    slots = place.shape[1]
    vmem = pl.BlockSpec(memory_space=pltpu.VMEM)
    out = [jax.ShapeDtypeStruct((slots * blk // LANES + 8, LANES), jnp.float32)]
    scratch = []
    if part == len(BOUNDS) - 2:
        out.append(jax.ShapeDtypeStruct((blk, slots), jnp.float32))
        scratch.append(pltpu.VMEM((slots, LANES), jnp.float32))
    operands = [place, resid, book] + ([before] if part else [])
    return pl.pallas_call(
        functools.partial(error_kernel, sub, part, blk),
        out_shape=tuple(out),
        in_specs=[
            pl.BlockSpec(memory_space=pltpu.SMEM),
            vmem,
            vmem,
            vmem,
        ][: len(operands)],
        out_specs=tuple(vmem for _ in out),
        scratch_shapes=scratch,
        compiler_params=pltpu.CompilerParams(vmem_limit_bytes=SMALL_VMEM),
        cost_estimate=pl.CostEstimate(
            flops=2 * 256 * codes * subspaces * GROUP * 3,
            bytes_accessed=width * GROUP * 2 * 3,
            transcendentals=0,
        ),
        name="row_errors",
    )(*operands)


def unpack_kernel(even_ref, own_ref, one_ref, two_ref, three_ref, total_ref, out_ref):
    sub = out_ref.shape[1]
    across = LANES // sub
    half = out_ref.shape[0] // across // 2
    even = even_ref[0] != 0
    one, three = one_ref[...], three_ref[...]
    packed = (own_ref[...] + jnp.where(even, three, one)) + (two_ref[...] + jnp.where(even, one, three))
    share = 1.0 / total_ref[0:1, 0:1]
    row = lax.broadcasted_iota(jnp.int32, (sub, sub), 0)
    lane = lax.broadcasted_iota(jnp.int32, (sub, sub), 1)
    for q in range(half):
        square = packed[q * sub : (q + 1) * sub]
        turned = square.T
        for a in range(across):
            at = slice(a * sub, (a + 1) * sub)
            here, flip = square[:, at], turned[at]
            diagonal = packed[half * sub + q : half * sub + q + 1, at]
            out_ref[q * across + a] = jnp.where(row <= lane, here, flip) * share
            other = jnp.where(row > lane, here, jnp.where(row < lane, flip, diagonal))
            out_ref[(half + q) * across + a] = other * share


def unpack_moments(terms, even, total, subspaces, sub):
    return pl.pallas_call(
        unpack_kernel,
        out_shape=jax.ShapeDtypeStruct((subspaces, sub, sub), jnp.float32),
        in_specs=[pl.BlockSpec(memory_space=pltpu.SMEM)] + [pl.BlockSpec(memory_space=pltpu.VMEM)] * 5,
        compiler_params=pltpu.CompilerParams(vmem_limit_bytes=SMALL_VMEM),
        name="unpack_moments",
    )(even, *terms, total)


def extended_book(codebook):
    values = codebook.astype(jnp.float32)
    rest = jnp.sum(jnp.square(values), axis=1)
    parts = []
    for _ in range(3):
        part = lax.reduce_precision(rest, 8, 7)
        parts.append(part)
        rest = rest - part
    parts = jnp.stack(parts, axis=2)
    parts = jnp.pad(parts, ((0, 0), (0, 0), (0, AUG - 3)))
    return jnp.concatenate([-2.0 * values.transpose(0, 2, 1), parts], axis=2).astype(jnp.bfloat16)


def body(vectors, row_list, block_owner, block_fill, old_centroids, codebook):
    devices = lax.axis_size("dev")
    blk = row_list.shape[0] // block_owner.shape[0]
    sub = codebook.shape[1]
    width = vectors.shape[1]
    book = extended_book(codebook)
    send = build_send(vectors, row_list, block_owner, block_fill, devices)
    recv = lax.all_to_all(send, "dev", split_axis=0, concat_axis=0, tiled=True)
    centroids, resid, place, packed, total = update_lists(recv, old_centroids, blk, sub)
    errors, slot_error = None, None
    for part in range(len(BOUNDS) - 1):
        out = row_errors(place, resid, book, errors, sub, blk, part)
        errors, slot_error = out[0], out[-1]

    me = lax.axis_index("dev")

    def shifted(values, stride, step, size):
        pairs = []
        for i in range(devices):
            digit = i // stride % size
            pairs.append((i, i + ((digit + step) % size - digit) * stride))
        return lax.ppermute(values, "dev", pairs)

    packed = packed + shifted(packed, 1, 1, 2)
    stride = 2
    while True:
        three, one, two = (shifted(packed, stride, k, 4) for k in (3, 1, 2))
        even = me // stride % 2 == 0
        terms = (packed, jnp.where(even, three, one), two, jnp.where(even, one, three))
        stride *= 4
        if stride >= devices:
            break
        packed = (terms[0] + terms[1]) + (terms[2] + terms[3])
    moments = unpack_moments((packed, one, two, three), even.astype(jnp.int32).reshape(1), total, codebook.shape[0], sub)
    return centroids, slot_error.T, moments


def solution(mesh):
    return jax.shard_map(
        body,
        mesh=mesh,
        in_specs=(P("dev", None), P("dev"), P("dev"), P("dev"), P("dev", None), P()),
        out_specs=(P("dev", None), P("dev", None), P()),
        check_vma=False,
    )
```

```python
import functools

import jax
import jax.numpy as jnp
from jax import lax
from jax.experimental import pallas as pl
from jax.experimental.pallas import tpu as pltpu
from jax.sharding import PartitionSpec as P

LANES = 128
META = 8
AUG = 16
GROUP = 256
VMEM = 37 * 1024 * 1024
LARGE_VMEM = 56 * 1024 * 1024
SMALL_VMEM = 10 * 1024 * 1024
BOUNDS = ((0, 0), (1, 8), (4, 8), (7, 4), (9, 0))


def send_kernel(
    blk, owner_hbm, fill_hbm, vec_ref, list_hbm, send_ref, owner_ref, fill_ref, list_ref, held, tiles, meta, sems
):
    blocks = owner_ref.shape[0]
    width = vec_ref.shape[1]
    small = [
        pltpu.make_async_copy(source, target, sems.at[blocks + 5 + i])
        for i, (source, target) in enumerate(
            ((owner_hbm, owner_ref), (fill_hbm, fill_ref), (list_hbm, list_ref))
        )
    ]
    for copy in small:
        copy.start()
    chunks = width // LANES
    span = LANES // blk
    me = lax.axis_index("dev")
    place = lax.rem(me, span)
    stages = held.shape[0]
    some = blocks // stages
    loads = [
        pltpu.make_async_copy(
            vec_ref.at[pl.ds(c * some * blk, some * blk), :], held.at[c], sems.at[blocks + 1 + c]
        )
        for c in range(stages)
    ]
    for load in loads:
        load.start()
    for copy in small:
        copy.wait()
    total = functools.reduce(lambda a, b: a + b, [fill_ref[b] for b in range(blocks)])
    rows = lax.broadcasted_iota(jnp.int32, (META, LANES), 0)
    lane = lax.broadcasted_iota(jnp.int32, (1, LANES), 1)
    base = jnp.where(rows == 3, total >> 8, jnp.where(rows == 4, total & 255, 0))
    meta[...] = jnp.broadcast_to(base.astype(jnp.float32).astype(jnp.bfloat16)[None], meta.shape)
    for b in range(blocks):
        line = list_ref[b // span : b // span + 1, :] + 1
        line = pltpu.roll(line, lax.rem(place + span - b % span, span) * blk, 1)
        kept = (lane // blk == place) & (lax.rem(lane, blk) < fill_ref[b])
        line = jnp.broadcast_to(jnp.where(kept, line, 0), (META, LANES))
        count = jnp.broadcast_to(jnp.where(lane == me, fill_ref[b], 0), (META, LANES))
        tile = jnp.where(
            rows == 0, line & 255, jnp.where(rows == 1, line >> 8, jnp.where(rows == 2, count, base))
        )
        meta[owner_ref[b]] = tile.astype(jnp.float32).astype(jnp.bfloat16)
    last = pltpu.make_async_copy(
        meta, send_ref.at[:, pl.ds(chunks * blk, META), :], sems.at[blocks]
    )
    last.start()
    copies = []
    for c in range(stages):
        loads[c].wait()
        for b in range(c * some, (c + 1) * some):
            at = slice((b - c * some) * blk, (b - c * some + 1) * blk)
            for j in range(chunks):
                tiles[b, j * blk : (j + 1) * blk, :] = held[c, at, j * LANES : (j + 1) * LANES]
            copy = pltpu.make_async_copy(
                tiles.at[b], send_ref.at[owner_ref[b], pl.ds(0, chunks * blk), :], sems.at[b]
            )
            copy.start()
            copies.append(copy)
    for copy in copies:
        copy.wait()
    last.wait()


def build_send(vectors, row_list, block_owner, block_fill, devices):
    rows, width = vectors.shape
    blocks = block_owner.shape[0]
    blk = rows // blocks
    height = width // LANES * blk
    return pl.pallas_call(
        functools.partial(send_kernel, blk),
        out_shape=jax.ShapeDtypeStruct((devices, height + META, LANES), jnp.bfloat16),
        in_specs=[pl.BlockSpec(memory_space=pl.ANY)] * 4,
        out_specs=pl.BlockSpec(memory_space=pl.ANY),
        scratch_shapes=[
            pltpu.SMEM((blocks,), jnp.int32),
            pltpu.SMEM((blocks,), jnp.int32),
            pltpu.VMEM((rows // LANES, LANES), jnp.int32),
            pltpu.VMEM((4, rows // 4, width), jnp.bfloat16),
            pltpu.VMEM((blocks, height, LANES), jnp.bfloat16),
            pltpu.VMEM((devices, META, LANES), jnp.bfloat16),
            pltpu.SemaphoreType.DMA((blocks + 8,)),
        ],
        compiler_params=pltpu.CompilerParams(vmem_limit_bytes=LARGE_VMEM),
        name="build_send",
    )(block_owner, block_fill, vectors, row_list.reshape(rows // LANES, LANES))


def update_kernel(
    blk, recv_ref, old_ref, cent_ref, turned, where_ref, packed_ref, total_ref,
    blocks, info, dense, hot, values, column, place_ref, sums, counts, parts, gram, sems,
):
    slots, height, _ = recv_ref.shape
    lists, width = old_ref.shape
    chunks = width // LANES
    span = LANES // blk
    some = slots // blocks.shape[0]
    rows = slots * blk

    notes = pltpu.make_async_copy(recv_ref.at[:, pl.ds(chunks * blk, META), :], info, sems.at[0])
    notes.start()

    def fetch(c):
        return pltpu.make_async_copy(
            recv_ref.at[pl.ds(c * some, some), pl.ds(0, chunks * blk), :], blocks.at[c], sems.at[1 + c]
        )

    for c in range(blocks.shape[0]):
        fetch(c).start()

    notes.wait()
    lines, seen = [], jnp.zeros((META, LANES), jnp.float32)
    for q in range(slots // span):
        note = info[q * span].astype(jnp.float32)
        for s in range(1, span):
            note = note + info[q * span + s].astype(jnp.float32)
        lines.append(note[0:1] + 256.0 * note[1:2])
        seen = seen + note
    fill = jnp.broadcast_to(seen[2:3], (8, LANES))
    before = lax.broadcasted_iota(jnp.int32, (slots, slots), 0)
    after = lax.broadcasted_iota(jnp.int32, (slots, slots), 1)
    start = jnp.dot(
        fill.astype(jnp.bfloat16),
        jnp.where(before < after, 1.0, 0.0).astype(jnp.bfloat16),
        preferred_element_type=jnp.float32,
    )
    which = lax.broadcasted_iota(jnp.int32, (8, slots), 0)
    where_ref[...] = jnp.where(which == 0, start, fill).astype(jnp.int32)
    mover = pltpu.make_async_copy(where_ref, place_ref, sems.at[0])
    mover.start()
    total_ref[...] = jnp.broadcast_to(seen[4:5] + 256.0 * seen[3:4], total_ref.shape)
    lines.append(jnp.zeros((LANES - len(lines), LANES), jnp.float32))
    column[...] = jnp.concatenate(lines, axis=0).T
    sums[...] = jnp.zeros_like(sums)
    counts[...] = jnp.zeros_like(counts)
    gram[...] = jnp.zeros_like(gram)
    mover.wait()

    lane = lax.broadcasted_iota(jnp.int32, (blk, LANES), 1)

    def pack(c, carry):
        fetch(c).wait()
        for s in range(some):
            at = pl.ds(place_ref[0, c * some + s], blk)
            for j in range(chunks):
                dense[j, at, :] = blocks[c, s, j * blk : (j + 1) * blk, :].astype(jnp.float32)
            ids = column[(s % span) * blk : (s % span + 1) * blk, :]
            dense[chunks, at, :] = jnp.where(lane == c * (some // span) + s // span, ids, 0.0)
        return carry

    for c in range(blocks.shape[0]):
        pack(c, 0)
    used = place_ref[0, slots - 1] + place_ref[1, slots - 1]
    for j in range(chunks + 1):
        dense[j, pl.ds(used, GROUP + blk), :] = jnp.zeros((GROUP + blk, LANES), jnp.float32)
    groups = jnp.maximum((used + GROUP - 1) // GROUP, 1)

    def prepare(g):
        at = pl.ds(pl.multiple_of(g * GROUP, GROUP), GROUP)
        code = jnp.sum(dense[chunks, at, :].T[0 : slots // span], axis=0, keepdims=True)
        ids = lax.broadcasted_iota(jnp.int32, (lists, GROUP), 0).astype(jnp.float32) + 1.0
        hot[g] = jnp.where(ids == code, 1.0, 0.0).astype(jnp.bfloat16)
        for j in range(chunks):
            piece = dense[j, at, :].astype(jnp.bfloat16)
            turned[g, j * LANES : (j + 1) * LANES, :] = piece.T
            values[g & 1, :, j * LANES : (j + 1) * LANES] = piece

    prepare(0)

    def add(g):
        chosen = hot[g]
        added = jnp.dot(chosen, values[g & 1], preferred_element_type=jnp.float32)
        part = chosen[:, 0:LANES].astype(jnp.float32)
        for k in range(1, GROUP // LANES):
            part = part + chosen[:, k * LANES : (k + 1) * LANES].astype(jnp.float32)
        return added, part

    def gather(g, carry):
        added, part = add(g)
        prepare(g + 1)
        sums[...] += added
        counts[...] += part
        return carry

    lax.fori_loop(0, groups - 1, gather, 0)
    added, part = add(groups - 1)
    share = 1.0 / (jnp.sum(counts[...] + part, axis=1, keepdims=True) + 1.0)
    cent = (sums[...] + added + old_ref[...]) * share
    sums[...] = cent
    write = pltpu.make_async_copy(sums, cent_ref, sems.at[0])
    write.start()
    flipped = cent.T
    head = flipped.astype(jnp.bfloat16)
    parts[:, 0:lists] = head
    parts[:, lists : 2 * lists] = (flipped - head.astype(jnp.float32)).astype(jnp.bfloat16)

    wide = 2 * LANES
    lane = lax.broadcasted_iota(jnp.int32, (1, GROUP), 1)

    def subtract(g):
        chosen = hot[g]
        weight = jnp.where(lane < used - g * GROUP, 1.0, 0.0)
        both = jnp.concatenate([chosen, chosen], axis=0)
        resids = []
        for j in range(width // wide):
            at = slice(j * wide, (j + 1) * wide)
            picked = jnp.dot(parts[at], both, preferred_element_type=jnp.float32)
            resids.append(((turned[g, at].astype(jnp.float32) - picked) * weight).astype(jnp.bfloat16))
        for j in range(width // wide):
            turned[g, j * wide : (j + 1) * wide] = resids[j]

    def multiply(g):
        resids = [turned[g, j * wide : (j + 1) * wide] for j in range(width // wide)]
        return [
            lax.dot_general(r, r, (((1,), (1,)), ((), ())), preferred_element_type=jnp.float32)
            for r in resids
        ]

    subtract(0)

    def encode(g, carry):
        squares = multiply(g)
        subtract(g + 1)
        for j in range(width // wide):
            gram[j] += squares[j]
        return carry

    lax.fori_loop(0, groups - 1, encode, 0)
    squares = multiply(groups - 1)
    for j in range(width // wide):
        gram[j] += squares[j]

    sub = (packed_ref.shape[0] - 8) // (chunks // 2)
    across = LANES // sub
    row = lax.broadcasted_iota(jnp.int32, (sub, LANES), 0)
    lane = lax.broadcasted_iota(jnp.int32, (sub, LANES), 1)
    squares = []
    for q in range(chunks):
        half = slice((q % 2) * LANES, (q % 2 + 1) * LANES)
        square = jnp.zeros((sub, LANES), jnp.float32)
        for a in range(across):
            top = ((q % 2) * across + a) * sub
            square = jnp.where(lane // sub == a, gram[q // 2, top : top + sub, half], square)
        squares.append(square)
    half = chunks // 2
    diagonals = []
    for q in range(half):
        packed_ref[q * sub : (q + 1) * sub, :] = jnp.where(
            row <= lane % sub, squares[q], squares[half + q]
        )
        diagonals.append(
            jnp.sum(jnp.where(row == lane % sub, squares[half + q], 0.0), axis=0, keepdims=True)
        )
    diagonals.append(jnp.zeros((8 - half, LANES), jnp.float32))
    packed_ref[half * sub :, :] = jnp.concatenate(diagonals, axis=0)

    write.wait()


def update_lists(recv, old, blk, sub):
    slots, height, _ = recv.shape
    lists, width = old.shape
    rows = slots * blk
    groups = rows // GROUP
    chunks = width // LANES
    return pl.pallas_call(
        functools.partial(update_kernel, blk),
        out_shape=(
            jax.ShapeDtypeStruct((lists, width), jnp.float32),
            jax.ShapeDtypeStruct((groups + 1, width, GROUP), jnp.bfloat16),
            jax.ShapeDtypeStruct((8, slots), jnp.int32),
            jax.ShapeDtypeStruct((chunks // 2 * sub + 8, LANES), jnp.float32),
            jax.ShapeDtypeStruct((8, LANES), jnp.float32),
        ),
        in_specs=[
            pl.BlockSpec(memory_space=pl.ANY),
            pl.BlockSpec(memory_space=pltpu.VMEM),
        ],
        out_specs=(
            pl.BlockSpec(memory_space=pl.ANY),
            pl.BlockSpec(memory_space=pltpu.VMEM),
            pl.BlockSpec(memory_space=pltpu.VMEM),
            pl.BlockSpec(memory_space=pltpu.VMEM),
            pl.BlockSpec(memory_space=pltpu.VMEM),
        ),
        scratch_shapes=[
            pltpu.VMEM((8, slots // 8, chunks * blk, LANES), jnp.bfloat16),
            pltpu.VMEM((slots, META, LANES), jnp.bfloat16),
            pltpu.VMEM((chunks + 1, rows + GROUP + blk, LANES), jnp.float32),
            pltpu.VMEM((groups + 1, lists, GROUP), jnp.bfloat16),
            pltpu.VMEM((2, GROUP, width), jnp.bfloat16),
            pltpu.VMEM((LANES, LANES), jnp.float32),
            pltpu.SMEM((8, slots), jnp.int32),
            pltpu.VMEM((lists, width), jnp.float32),
            pltpu.VMEM((lists, LANES), jnp.float32),
            pltpu.VMEM((width, 2 * lists), jnp.bfloat16),
            pltpu.VMEM((width // (2 * LANES), 2 * LANES, 2 * LANES), jnp.float32),
            pltpu.SemaphoreType.DMA((10,)),
        ],
        compiler_params=pltpu.CompilerParams(vmem_limit_bytes=VMEM),
        name="update_lists",
    )(recv, old)


def error_kernel(sub, part, blk, place_ref, resid_ref, book_ref, *rest):
    before_ref, error_ref = rest[:2] if part else (None, rest[0])
    slot_ref, lines = rest[2:4] if part == len(BOUNDS) - 2 else (None, None)
    subspaces = book_ref.shape[0]
    slots = place_ref.shape[1]
    width = subspaces * sub
    used = place_ref[0, slots - 1] + place_ref[1, slots - 1]
    groups = (used + GROUP - 1) // GROUP
    first, last = (
        (groups * top + rest) // BOUNDS[-1][0] for top, rest in (BOUNDS[part], BOUNDS[part + 1])
    )
    error_ref[...] = before_ref[...] if part else jnp.zeros_like(error_ref)

    ones = jnp.ones((AUG, GROUP), jnp.bfloat16)

    def visit(g, carry):
        norm = jnp.zeros((8, GROUP), jnp.float32)
        least = jnp.zeros((1, GROUP), jnp.float32)
        for m in range(subspaces):
            piece = resid_ref[g, m * sub : (m + 1) * sub, :]
            long = piece.astype(jnp.float32)
            square = long * long
            for k in range(sub // 8):
                norm = norm + square[k * 8 : (k + 1) * 8]
            distance = jnp.dot(
                book_ref[m],
                jnp.concatenate([piece, ones], axis=0),
                preferred_element_type=jnp.float32,
            )
            least = least + jnp.min(distance, axis=0, keepdims=True)
        error = (least + jnp.sum(norm, axis=0, keepdims=True)) / width
        for k in range(GROUP // LANES):
            error_ref[pl.ds(g * (GROUP // LANES) + k, 1), :] = error[:, k * LANES : (k + 1) * LANES]
        return carry

    lax.fori_loop(first, last, visit, 0)

    if slot_ref is not None:
        lane = lax.broadcasted_iota(jnp.int32, (1, LANES), 1)
        for s in range(slots):
            start = place_ref[0, s]
            line = lax.shift_right_logical(start, LANES.bit_length() - 1)
            shift = start & (LANES - 1)
            window = jnp.where(
                lane >= shift, error_ref[pl.ds(line, 1), :], error_ref[pl.ds(line + 1, 1), :]
            )
            window = pltpu.roll(window, (LANES - shift) & (LANES - 1), 1)
            window = jnp.where(lane < place_ref[1, s], window, 0.0)
            lines[s : s + 1, :] = window
        slot_ref[...] = lines[...].T[0:blk]


def row_errors(place, resid, book, before, sub, blk, part):
    groups, width, _ = resid.shape
    subspaces, codes, depth = book.shape
    slots = place.shape[1]
    vmem = pl.BlockSpec(memory_space=pltpu.VMEM)
    out = [jax.ShapeDtypeStruct((slots * blk // LANES + 8, LANES), jnp.float32)]
    scratch = []
    if part == len(BOUNDS) - 2:
        out.append(jax.ShapeDtypeStruct((blk, slots), jnp.float32))
        scratch.append(pltpu.VMEM((slots, LANES), jnp.float32))
    operands = [place, resid, book] + ([before] if part else [])
    return pl.pallas_call(
        functools.partial(error_kernel, sub, part, blk),
        out_shape=tuple(out),
        in_specs=[
            pl.BlockSpec(memory_space=pltpu.SMEM),
            vmem,
            vmem,
            vmem,
        ][: len(operands)],
        out_specs=tuple(vmem for _ in out),
        scratch_shapes=scratch,
        compiler_params=pltpu.CompilerParams(vmem_limit_bytes=SMALL_VMEM),
        cost_estimate=pl.CostEstimate(
            flops=2 * 256 * codes * subspaces * GROUP * 3,
            bytes_accessed=width * GROUP * 2 * 3,
            transcendentals=0,
        ),
        name="row_errors",
    )(*operands)


def unpack_kernel(even_ref, own_ref, one_ref, two_ref, three_ref, total_ref, out_ref):
    sub = out_ref.shape[1]
    across = LANES // sub
    half = out_ref.shape[0] // across // 2
    even = even_ref[0] != 0
    one, three = one_ref[...], three_ref[...]
    packed = (own_ref[...] + jnp.where(even, three, one)) + (two_ref[...] + jnp.where(even, one, three))
    share = 1.0 / total_ref[0:1, 0:1]
    row = lax.broadcasted_iota(jnp.int32, (sub, sub), 0)
    lane = lax.broadcasted_iota(jnp.int32, (sub, sub), 1)
    for q in range(half):
        square = packed[q * sub : (q + 1) * sub]
        turned = square.T
        for a in range(across):
            at = slice(a * sub, (a + 1) * sub)
            here, flip = square[:, at], turned[at]
            diagonal = packed[half * sub + q : half * sub + q + 1, at]
            out_ref[q * across + a] = jnp.where(row <= lane, here, flip) * share
            other = jnp.where(row > lane, here, jnp.where(row < lane, flip, diagonal))
            out_ref[(half + q) * across + a] = other * share


def unpack_moments(terms, even, total, subspaces, sub):
    return pl.pallas_call(
        unpack_kernel,
        out_shape=jax.ShapeDtypeStruct((subspaces, sub, sub), jnp.float32),
        in_specs=[pl.BlockSpec(memory_space=pltpu.SMEM)] + [pl.BlockSpec(memory_space=pltpu.VMEM)] * 5,
        compiler_params=pltpu.CompilerParams(vmem_limit_bytes=SMALL_VMEM),
        name="unpack_moments",
    )(even, *terms, total)


def extended_book(codebook):
    values = codebook.astype(jnp.float32)
    rest = jnp.sum(jnp.square(values), axis=1)
    parts = []
    for _ in range(3):
        part = lax.reduce_precision(rest, 8, 7)
        parts.append(part)
        rest = rest - part
    parts = jnp.stack(parts, axis=2)
    parts = jnp.pad(parts, ((0, 0), (0, 0), (0, AUG - 3)))
    return jnp.concatenate([-2.0 * values.transpose(0, 2, 1), parts], axis=2).astype(jnp.bfloat16)


def body(vectors, row_list, block_owner, block_fill, old_centroids, codebook):
    devices = lax.axis_size("dev")
    blk = row_list.shape[0] // block_owner.shape[0]
    sub = codebook.shape[1]
    width = vectors.shape[1]
    book = extended_book(codebook)
    send = build_send(vectors, row_list, block_owner, block_fill, devices)
    recv = lax.all_to_all(send, "dev", split_axis=0, concat_axis=0, tiled=True)
    centroids, resid, place, packed, total = update_lists(recv, old_centroids, blk, sub)
    errors, slot_error = None, None
    for part in range(len(BOUNDS) - 1):
        out = row_errors(place, resid, book, errors, sub, blk, part)
        errors, slot_error = out[0], out[-1]

    me = lax.axis_index("dev")

    def shifted(values, stride, step, size):
        pairs = []
        for i in range(devices):
            digit = i // stride % size
            pairs.append((i, i + ((digit + step) % size - digit) * stride))
        return lax.ppermute(values, "dev", pairs)

    packed = packed + shifted(packed, 1, 1, 2)
    stride = 2
    while True:
        three, one, two = (shifted(packed, stride, k, 4) for k in (3, 1, 2))
        even = me // stride % 2 == 0
        terms = (packed, jnp.where(even, three, one), two, jnp.where(even, one, three))
        stride *= 4
        if stride >= devices:
            break
        packed = (terms[0] + terms[1]) + (terms[2] + terms[3])
    moments = unpack_moments((packed, one, two, three), even.astype(jnp.int32).reshape(1), total, codebook.shape[0], sub)
    return centroids, slot_error.T, moments


def solution(mesh):
    return jax.shard_map(
        body,
        mesh=mesh,
        in_specs=(P("dev", None), P("dev"), P("dev"), P("dev"), P("dev", None), P()),
        out_specs=(P("dev", None), P("dev", None), P()),
        check_vma=False,
    )
```
